512 devices in a mesh: seq: 64 (over y, x, z_lo), head: 8 (over z_hi, core).
Axes of the slice: x: 4, y: 4, z: 16 (z_hi: 4, z_lo: 4; z = z_hi * 4 + z_lo), core: 2. Of those that a mesh axis runs over, the one named last changes fastest.
Arguments:
- inputs: bfloat16 [16384, 4096], P('seq', 'head'), may hold values from -6 to 6
- gating: bfloat16 [16384, 4096], P('seq', 'head'), may hold values from -6 to 6
- state_proj: bfloat16 [16384, 256], P('seq'), may hold values from -6 to 6
- conv_inputs: float32 [4, 4096], P(None, 'head'), may hold values from -3 to 3
- conv_state: float32 [4, 256], replicated, may hold values from -3 to 3
- step_raw: bfloat16 [64, 16384], P('head', 'seq'), may hold values from -3 to 3
- step_bias: float32 [64], P('head'), may hold values from -9 to -2
- decay_log: float32 [64], P('head'), may hold values from -8 to 1.5
- skip_gain: float32 [64], P('head'), may hold values from 0.5 to 1.5
- norm_gain: float32 [4096], P('head'), may hold values from 0.5 to 1.5
- boundaries: int32 [8], replicated, may hold values from 1 to 16383, as said below
Outputs:
- mixed_out: bfloat16 [16384, 4096], P('seq', 'head')
The draws below stay inside these ranges and needn't reach their ends.
Inputs may be any that keep to these rules, and one draw needn't show every extreme that they name: `boundaries`: 8 distinct token positions, one of them 16384 - 1.
All inputs are finite; a program needn't handle non-finite values.
Results may differ from the reference program's by a relative error of at most 0.015.
Values may be sent and summed in bfloat16 or wider, within the bound.
A program may use at most 128 MiB of HBM per device.

```python
import math
from functools import partial
import jax
import jax.numpy as jnp
from jax import lax

HEADS = 64
HEADDIM = 64
STATE = 128
GROUP = 128
CONV = 4
BOUNDS = 8
TOK_DEV = 256
LENGTH = 16384
CHANNELS = 4096


def head_rates(key, slow_share, middle_share):
    picker = jax.random.uniform(jax.random.fold_in(key, 11), (HEADS,))
    slow_heads = picker < slow_share
    middle_heads = (picker >= slow_share) & (picker < slow_share + middle_share)
    rough_step = jnp.exp(jax.random.uniform(jax.random.fold_in(key, 12), (HEADS,), minval=-0.7, maxval=0.7))
    rough_rate = jnp.exp(jax.random.uniform(jax.random.fold_in(key, 13), (HEADS,), minval=-0.5, maxval=0.5))
    slow_step = 3.0 / (11.0 * math.sqrt(LENGTH)) * rough_step
    middle_step = 0.02 * rough_step
    fast_step = 0.04 * rough_step
    step_size = jnp.where(slow_heads, slow_step, jnp.where(middle_heads, middle_step, fast_step))
    slow_rate = 0.6 / (LENGTH * step_size)
    middle_rate = 0.8 / (TOK_DEV * step_size)
    fast_rate = 1.0 / (40.0 * step_size)
    rate = jnp.where(slow_heads, slow_rate, jnp.where(middle_heads, middle_rate, fast_rate)) * rough_rate
    return (step_size, rate)


def draw_step_bias(key, part):
    step_size, rate = head_rates(key, 0.4, 0.3)
    return jnp.log(jnp.expm1(step_size)).astype(jnp.float32)


def draw_decay_log(key, part):
    step_size, rate = head_rates(key, 0.4, 0.3)
    return jnp.log(rate).astype(jnp.float32)


def draw_step_raw(key, part):
    key = jax.random.fold_in(key, 31)
    shard_count = LENGTH // TOK_DEV
    offsets = jax.random.uniform(jax.random.fold_in(key, 1), (HEADS, shard_count), minval=-2.6, maxval=1.4)
    spread = jnp.repeat(offsets, TOK_DEV, axis=1)
    noise = 0.4 * jax.random.normal(jax.random.fold_in(key, 2), (HEADS, LENGTH))
    return jnp.clip(spread + noise, -3.0, 3.0).astype(jnp.bfloat16)


def draw_boundaries(key, part):
    picked = jax.random.choice(jax.random.fold_in(key, 21), LENGTH - 2, (BOUNDS - 1,), replace=False)
    last_one = jnp.full((1,), LENGTH - 1, jnp.int32)
    return jnp.concatenate([(picked + 1).astype(jnp.int32), last_one]).astype(jnp.int32)


def block_scale(stream_key, dims, pieces, smallest, high):
    gain = 1.0
    for position, blocks in pieces:
        heights = jax.random.uniform(jax.random.fold_in(jax.random.fold_in(stream_key, 6), position), (blocks,), jnp.float32, smallest / len(pieces), high / len(pieces))
        gain = gain * jnp.repeat(jnp.exp(heights), dims[position] // blocks).reshape((-1,) + (1,) * (len(dims) - 1 - position))
    return gain


def gaussian(own_key, extent, width, reach, pieces=(), dtype=jnp.bfloat16):
    entries = width * jax.random.normal(own_key, extent, jnp.float32)
    if pieces:
        entries = entries * block_scale(own_key, extent, pieces, -0.22, 0.18)
    return jnp.clip(entries, -reach, reach).astype(dtype)


def setup_inputs(seed: int = 0) -> dict:
    arg_keys = jax.random.split(jax.random.key(seed), 12)
    inputs = gaussian(arg_keys[0], (LENGTH, CHANNELS), 1.0, 6.0, ((0, 64), (1, 8)))
    gating = gaussian(arg_keys[1], (LENGTH, CHANNELS), 1.0, 6.0, ((0, 64), (1, 8)))
    state_proj = gaussian(arg_keys[2], (LENGTH, 2 * STATE), 1.0, 6.0, ((0, 64),))
    conv_inputs = gaussian(arg_keys[3], (CONV, CHANNELS), CONV ** -0.5, 3.0, ((1, 8),), jnp.float32)
    conv_state = gaussian(arg_keys[4], (CONV, 2 * STATE), CONV ** -0.5, 3.0, (), jnp.float32)
    step_raw = draw_step_raw(jax.random.fold_in(arg_keys[11], 71), 0)
    step_bias = draw_step_bias(jax.random.fold_in(arg_keys[11], 71), 0)
    decay_log = draw_decay_log(jax.random.fold_in(arg_keys[11], 71), 0)
    skip_gain = jnp.clip(0.5 + 1.0 * jax.random.uniform(arg_keys[8], (HEADS,), jnp.float32) ** block_scale(arg_keys[8], (HEADS,), ((0, 8),), -0.2, 0.2), 0.5, 1.5)
    norm_gain = jnp.clip(1.0 + 0.1 * jax.random.normal(arg_keys[9], (CHANNELS,), jnp.float32), 0.5, 1.5)
    boundaries = draw_boundaries(jax.random.fold_in(arg_keys[11], 71), 0)
    return dict(inputs=inputs, gating=gating, state_proj=state_proj, conv_inputs=conv_inputs, conv_state=conv_state, step_raw=step_raw, step_bias=step_bias, decay_log=decay_log, skip_gain=skip_gain, norm_gain=norm_gain, boundaries=boundaries)


def both_convs(padded, taps, tok_rows):
    taps_count = taps.shape[0]
    forward = jnp.zeros((tok_rows, padded.shape[1]), jnp.float32)
    backward = jnp.zeros((tok_rows, padded.shape[1]), jnp.float32)
    for offset in range(taps_count):
        lower = taps_count - 1 - offset
        upper = taps_count - 1 + offset
        forward = forward + taps[offset] * padded[lower:lower + tok_rows].astype(jnp.float32)
        backward = backward + taps[offset] * padded[upper:upper + tok_rows].astype(jnp.float32)
    return (jax.nn.silu(forward).astype(jnp.bfloat16), jax.nn.silu(backward).astype(jnp.bfloat16))

def contig_labels(positions, boundaries):
    return lax.optimization_barrier(jnp.sum((boundaries[None, :] <= positions[:, None]).astype(jnp.int32), axis=1)).astype(jnp.int32)

def group_step(skip_gain, carry, piece):
    running, label_prev = carry
    blocked_x, b_block, c_block, step_size, decays, labels_blk = piece
    group_len = labels_blk.shape[0]
    log_cum = jnp.cumsum(decays, axis=-1)
    keep_mask = labels_blk == label_prev
    positions = jnp.arange(group_len)
    same_mask = (labels_blk[:, None] == labels_blk[None, :]) & (positions[:, None] >= positions[None, :])
    scores = jnp.dot(c_block, b_block.T, preferred_element_type=jnp.float32)
    log_gap = log_cum[:, :, None] - log_cum[:, None, :]
    weight = jnp.where(same_mask[None], jnp.exp(jnp.where(same_mask[None], log_gap, 0.0)), 0.0)
    mixing = (scores[None] * weight * step_size[:, None, :]).astype(jnp.bfloat16)
    mixing = lax.optimization_barrier(mixing).astype(jnp.float32)
    x_float = blocked_x.astype(jnp.float32)
    intra_out = jnp.einsum('hij,jhp->ihp', mixing, x_float)
    state_low = lax.optimization_barrier(running.astype(jnp.bfloat16)).astype(jnp.float32)
    inter_out = jnp.einsum('in,hnp->ihp', c_block.astype(jnp.float32), state_low)
    inflow = jnp.where(keep_mask[None], jnp.exp(log_cum), 0.0)
    output = intra_out + inter_out * inflow.T[:, :, None] + skip_gain[None, :, None] * x_float
    tail_scale = jnp.where(labels_blk[None] == labels_blk[-1], jnp.exp(log_cum[:, -1:] - log_cum), 0.0) * step_size
    scaled_b = (tail_scale[:, :, None] * b_block[None].astype(jnp.float32)).astype(jnp.bfloat16)
    scaled_b = lax.optimization_barrier(scaled_b).astype(jnp.float32)
    new_states = jnp.einsum('hjn,jhp->hnp', scaled_b, x_float)
    passes = jnp.where(keep_mask[-1], jnp.exp(log_cum[:, -1]), 0.0)
    running = passes[:, None, None] * running + new_states
    return ((running, labels_blk[-1]), output.astype(jnp.bfloat16))

def run_strand(x_vals, s_vals, step_size, decays, labels, skip_gain):
    total_len = x_vals.shape[0]
    group_count = total_len // GROUP
    blocked_x = x_vals.reshape(group_count, GROUP, HEADS, HEADDIM)
    b_blocks = s_vals[:, :STATE].reshape(group_count, GROUP, STATE)
    c_blocks = s_vals[:, STATE:].reshape(group_count, GROUP, STATE)
    step_blocks = step_size.reshape(HEADS, group_count, GROUP).transpose(1, 0, 2)
    decay_blocks = decays.reshape(HEADS, group_count, GROUP).transpose(1, 0, 2)
    label_blocks = labels.reshape(group_count, GROUP)
    start = (jnp.zeros((HEADS, STATE, HEADDIM), jnp.float32), labels[0])
    unused, outputs = lax.scan(partial(group_step, skip_gain), start, (blocked_x, b_blocks, c_blocks, step_blocks, decay_blocks, label_blocks))
    return outputs.reshape(total_len, HEADS * HEADDIM)

def reference(inputs, gating, state_proj, conv_inputs, conv_state, step_raw, step_bias, decay_log, skip_gain, norm_gain, boundaries):
    total_len = inputs.shape[0]
    margin = ((CONV - 1, CONV - 1), (0, 0))
    fore_x, back_x = both_convs(jnp.pad(inputs, margin), conv_inputs, total_len)
    fore_s, back_s = both_convs(jnp.pad(state_proj, margin), conv_state, total_len)
    step_size = jax.nn.softplus(step_raw.astype(jnp.float32) + step_bias[:, None])
    decays = -jnp.exp(decay_log)[:, None] * step_size
    labels = contig_labels(jnp.arange(total_len).astype(jnp.int32), boundaries)
    fore_out = run_strand(fore_x, fore_s, step_size, decays, labels, skip_gain)
    back_out = jnp.flip(run_strand(jnp.flip(back_x, 0), jnp.flip(back_s, 0), jnp.flip(step_size, 1), jnp.flip(decays, 1), jnp.flip(labels, 0), skip_gain), 0)
    mixed = (fore_out.astype(jnp.float32) + back_out.astype(jnp.float32)) * jax.nn.silu(gating.astype(jnp.float32))
    scale = lax.rsqrt(lax.optimization_barrier(jnp.mean(mixed * mixed, axis=1, keepdims=True)) + 1e-05)
    return (mixed * scale * norm_gain[None, :]).astype(jnp.bfloat16)
```

```python
import functools

import jax
import jax.numpy as jnp
from jax import lax
from jax.experimental import pallas as pl
from jax.experimental.pallas import tpu as pltpu
from jax.sharding import PartitionSpec as P

MESH = pl.DeviceIdType.MESH
LOG2E = 1.4426950408889634
NEG = -1e30
F32 = jnp.float32
BF16 = jnp.bfloat16
TOK = 256
GROUP = 128
PAIRS = 4
TILES = 64
PAD = 8


def mm(a, b):
    return lax.dot_general(a, b, (((1,), (0,)), ((), ())), preferred_element_type=F32)


def mm_nt(a, b):
    return lax.dot_general(a, b, (((1,), (1,)), ((), ())), preferred_element_type=F32)


def mm_exact(a, b):
    return lax.dot_general(
        a, b, (((1,), (0,)), ((), ())), preferred_element_type=F32, precision=lax.Precision.HIGHEST
    )


def gate(half):
    return half + half * jnp.tanh(half)


def kernel(
    n,
    nh,
    channels,
    x_hbm,
    g_hbm,
    s_hbm,
    cx_hbm,
    cs_hbm,
    raw_hbm,
    gain_hbm,
    bias,
    dlog,
    skip,
    bounds,
    out_hbm,
    xb,
    gb,
    sb,
    cx,
    cs,
    raw,
    gain,
    xl,
    xr,
    sl,
    sr,
    xp,
    sp,
    xd,
    cv,
    bt,
    gm,
    mk,
    kp,
    st,
    yv,
    infl,
    sg,
    dsend,
    drecv,
    sbuf,
    rbuf,
    ebuf,
    fbuf,
    hbuf,
    ob,
    in_sem,
    out_sem,
    halo_send,
    halo_recv,
    fac_sem,
    tile_sem,
    back_sem,
    head_sem,
):
    seq = lax.axis_index("seq")
    head = lax.axis_index("head")
    tp = TILES // n
    fj = 1 if tp == 1 else PAIRS

    def load(i, src, dst):
        copy = pltpu.make_async_copy(src, dst, in_sem.at[i])
        copy.start()
        return copy

    load_raw = load(0, raw_hbm, raw)
    load_s = load(1, s_hbm, sb)
    load_cs = load(2, cs_hbm, cs)
    load_x = load(3, x_hbm, xb)
    load_cx = load(4, cx_hbm, cx)
    load_g = load(5, g_hbm, gb)
    load_gain = load(6, gain_hbm, gain)

    barrier = pltpu.get_barrier_semaphore()

    def greet(d, carry):
        pl.semaphore_signal(
            barrier, inc=1, device_id=(lax.rem(seq + d, n), head), device_id_type=MESH
        )
        return carry

    lax.fori_loop(1, n, greet, 0)

    def greet_head(d, carry):
        pl.semaphore_signal(
            barrier, inc=1, device_id=(seq, lax.rem(head + d, nh)), device_id_type=MESH
        )
        return carry

    lax.fori_loop(1, nh, greet_head, 0)

    load_raw.wait()
    sub = lax.broadcasted_iota(jnp.int32, (8, 128), 0)
    lane = lax.broadcasted_iota(jnp.int32, (1, 128), 1)
    left = lane < 64
    bias_col = jnp.zeros((8, 128), F32)
    rate_col = jnp.zeros((8, 128), F32)
    for h in range(8):
        bias_col = jnp.where(sub == h, bias[h], bias_col)
        rate_col = jnp.where(sub == h, dlog[h], rate_col)
    rate_col = -LOG2E * jnp.exp(rate_col)
    steps = []
    for b in range(2):
        z = raw[:, b * 128 : (b + 1) * 128].astype(F32) + bias_col
        small = jnp.exp(-jnp.abs(z))
        one = 1.0 + small
        exact = jnp.where(one == 1.0, small, jnp.log(one) * (small / jnp.where(one == 1.0, 1.0, one - 1.0)))
        steps.append(jnp.maximum(z, 0.0) + exact)
    decay = jnp.concatenate([steps[0] * rate_col, steps[1] * rate_col], axis=0)
    log_step = jnp.log(jnp.concatenate(steps, axis=0)) * LOG2E
    row_i = lax.broadcasted_iota(jnp.int32, (128, 128), 0)
    col_i = lax.broadcasted_iota(jnp.int32, (128, 128), 1)
    cum_f = mm_exact(decay, (row_i <= col_i).astype(F32))
    cum_b = mm_exact(decay, (row_i >= col_i).astype(F32))
    cums = (cum_f, cum_b)
    cols = jnp.transpose(jnp.concatenate([cum_f, cum_b, jnp.zeros((96, 128), F32)], axis=0))
    minus = (cum_f - log_step, cum_b - log_step)

    base = seq * TOK

    def label(position):
        count = jnp.zeros_like(position)
        for i in range(8):
            count = count + (bounds[i] <= position).astype(jnp.int32)
        return count

    first = (label(base), label(base + 128))
    last = (label(base + 127), label(base + 255))
    prev = (label(base - 1), last[0])
    after = (first[1], label(base + 256))
    ends = []
    passes = []
    tails = []
    for s in range(2):
        ends.append([])
        passes.append([])
        tails.append([])
        for b in range(2):
            block = cums[s][b * 8 : (b + 1) * 8]
            end = jnp.broadcast_to(block[:, 127:128] if s == 0 else block[:, 0:1], (8, 128))
            ends[s].append(end)
            end_label = last[b] if s == 0 else first[b]
            outside = prev[b] if s == 0 else after[b]
            passes[s].append(jnp.where(end_label == outside, jnp.exp2(end), 0.0))
            labels = label(base + b * 128 + lax.broadcasted_iota(jnp.int32, (8, 128), 1))
            tails[s].append(
                jnp.where(
                    labels == end_label, jnp.exp2(end - minus[s][b * 8 : (b + 1) * 8]), 0.0
                )
            )
            tok = label(base + b * 128 + row_i)
            other = labels[0:1]
            order = row_i >= col_i if s == 0 else row_i <= col_i
            mk[s * 2 + b] = jnp.where((tok == other) & order, 0.0, NEG)
            kp[s * 2 + b] = jnp.where(tok == outside, 0.0, NEG)

    def spread(column, j):
        return jnp.where(left, column[2 * j : 2 * j + 1], column[2 * j + 1 : 2 * j + 2])

    for s in range(2):
        factor = passes[s][0] * passes[s][1]
        for j in range(PAIRS):
            dsend[s * PAIRS + j] = spread(factor, j)

    load_s.wait()
    load_cs.wait()
    load_x.wait()
    load_cx.wait()

    pl.semaphore_wait(barrier, n - 1 + nh - 1)

    right_dev = (lax.rem(seq + 1, n), head)
    left_dev = (lax.rem(seq + n - 1, n), head)
    halos = []
    for i, (src, dst, dev) in enumerate(
        (
            (x_hbm.at[TOK - 16 : TOK], xl, right_dev),
            (s_hbm.at[TOK - 16 : TOK], sl, right_dev),
            (x_hbm.at[0:16], xr, left_dev),
            (s_hbm.at[0:16], sr, left_dev),
        )
    ):
        copy = pltpu.make_async_remote_copy(
            src_ref=src,
            dst_ref=dst,
            send_sem=halo_send.at[i],
            recv_sem=halo_recv.at[i],
            device_id=dev,
            device_id_type=MESH,
        )
        copy.start()
        halos.append(copy)

    def send_factor(d, carry):
        p = lax.rem(seq + d, n)
        tile = p * tp
        strand = tile // 32
        at = strand * PAIRS + (lax.rem(tile, PAIRS) if fj == 1 else 0)
        pltpu.make_async_remote_copy(
            src_ref=dsend.at[pl.ds(at, fj)],
            dst_ref=drecv.at[seq],
            send_sem=fac_sem.at[0],
            recv_sem=fac_sem.at[1],
            device_id=(p, head),
            device_id_type=MESH,
        ).start()
        return carry

    lax.fori_loop(1, n, send_factor, 0)
    tile0 = seq * tp
    at0 = (tile0 // 32) * PAIRS + (lax.rem(tile0, PAIRS) if fj == 1 else 0)
    drecv[seq] = dsend[pl.ds(at0, fj)]

    xp[PAD : PAD + TOK] = xb[...].astype(F32)
    sp[PAD : PAD + TOK] = sb[...].astype(F32)

    def conv(padded, taps, c, r0, rows, s):
        lanes = slice(c * 128, (c + 1) * 128)
        total = None
        for k in range(4):
            shift = -k if s == 0 else k
            term = (0.5 * taps[k : k + 1, lanes]) * padded[
                PAD + r0 + shift : PAD + r0 + shift + rows, lanes
            ]
            total = term if total is None else total + term
        return gate(total)

    def conv_x(j, r0, rows, s):
        v = conv(xp, cx, j, r0, rows, s)
        b = r0 // 128
        r = r0 - b * 128
        xd[s * 2 + b, j, r : r + rows] = jnp.where(left, v, 0.0).astype(BF16)
        xd[s * 2 + b, j, 128 + r : 128 + r + rows] = jnp.where(left, 0.0, v).astype(BF16)

    def conv_s(c, r0, rows, s):
        v = conv(sp, cs, c, r0, rows, s)
        b = r0 // 128
        r = r0 - b * 128
        cv[s * 2 + b, c, r : r + rows] = v.astype(BF16)

    inner = (
        (0, ((16, 48), (64, 64), (128, 64), (192, 64))),
        (1, ((0, 64), (64, 64), (128, 64), (192, 48))),
    )
    edges = ((0, 0), (1, TOK - 16))
    for c in range(2):
        for s, chunks in inner:
            for r0, rows in chunks:
                conv_s(c, r0, rows, s)
    for j in range(PAIRS):
        for s, chunks in inner:
            for r0, rows in chunks:
                conv_x(j, r0, rows, s)

    for copy in halos:
        copy.wait()
    has_left = seq > 0
    has_right = seq < n - 1
    xp[0:PAD] = jnp.where(has_left, xl[...].astype(F32)[16 - PAD :], 0.0)
    xp[PAD + TOK : PAD + TOK + PAD] = jnp.where(has_right, xr[...].astype(F32)[:PAD], 0.0)
    sp[0:PAD] = jnp.where(has_left, sl[...].astype(F32)[16 - PAD :], 0.0)
    sp[PAD + TOK : PAD + TOK + PAD] = jnp.where(has_right, sr[...].astype(F32)[:PAD], 0.0)
    for s, r0 in edges:
        for c in range(2):
            conv_s(c, r0, 16, s)
        for j in range(PAIRS):
            conv_x(j, r0, 16, s)

    for q in range(4):
        bt[q] = jnp.transpose(cv[q, 0].astype(F32))
    for j in range(PAIRS):
        for s in range(2):
            parts = []
            for b in range(2):
                q = s * 2 + b
                scaled = jnp.concatenate(
                    [bt[q] * tails[s][b][2 * j + k : 2 * j + k + 1] for k in range(2)], axis=1
                ).astype(BF16)
                parts.append(mm(scaled, xd[q, j]))
            early, late = (parts[0], parts[1]) if s == 0 else (parts[1], parts[0])
            st[s, j] = early.astype(BF16)
            total = (spread(passes[s][1 - s], j) * early + late).astype(BF16)
            for i in range(8):
                t = s * 32 + i * PAIRS + j
                sbuf[t // tp, t % tp] = total[i * 16 : (i + 1) * 16]

    def send_tiles(d, carry):
        p = lax.rem(seq + d, n)
        pltpu.make_async_remote_copy(
            src_ref=sbuf.at[p],
            dst_ref=rbuf.at[seq],
            send_sem=tile_sem.at[0],
            recv_sem=tile_sem.at[1],
            device_id=(p, head),
            device_id_type=MESH,
        ).start()
        return carry

    lax.fori_loop(1, n, send_tiles, 0)
    rbuf[seq] = sbuf[seq]

    def within(b):
        if b == 0:
            for q in range(4):
                gm[q] = mm_nt(cv[q, 1], cv[q, 0])
        for j in range(PAIRS):
            total = None
            for s in range(2):
                q = s * 2 + b
                wide = []
                parts = []
                for k in range(2):
                    h = 2 * j + k
                    at = s * 16 + b * 8 + h
                    column = jnp.broadcast_to(cols[:, at : at + 1], (128, 128))
                    wide.append(column)
                    row = minus[s][b * 8 + h : b * 8 + h + 1]
                    parts.append((jnp.exp2(column - row + mk[q]) * gm[q]).astype(BF16))
                values = xd[q, j]
                term = mm(jnp.concatenate(parts, axis=1), values)
                sk = jnp.where(left, skip[2 * j], skip[2 * j + 1])
                term = term + sk * (values[:128].astype(F32) + values[128:].astype(F32))
                flow = jnp.exp2(jnp.where(left, wide[0], wide[1]) + kp[q])
                if b != s:
                    term = term + flow * mm(cv[q, 1], st[s, j])
                    flow = flow * spread(passes[s][s], j)
                infl[s, j, b * 128 : (b + 1) * 128] = flow
                total = term if total is None else total + term
            yv[j, b * 128 : (b + 1) * 128] = total

    within(0)

    def wait_all(sem, ref):
        pltpu.make_async_copy(ref, ref, sem).wait()

    wait_all(fac_sem.at[0], drecv.at[pl.ds(0, n - 1)])
    wait_all(fac_sem.at[1], drecv.at[pl.ds(0, n - 1)])
    wait_all(tile_sem.at[0], rbuf.at[pl.ds(0, n - 1)])
    wait_all(tile_sem.at[1], rbuf.at[pl.ds(0, n - 1)])

    reverse = tile0 >= 32

    def scan(i, carry):
        k = jnp.where(reverse, n - 1 - i, i)
        new = []
        for t in range(tp):
            ebuf[k, t] = carry[t].astype(BF16)
            new.append(drecv[k, t % fj] * carry[t] + rbuf[k, t].astype(F32))
        return tuple(new)

    lax.fori_loop(0, n, scan, tuple(jnp.zeros((16, 128), F32) for _ in range(tp)))

    def send_back(d, carry):
        p = lax.rem(seq + d, n)
        pltpu.make_async_remote_copy(
            src_ref=ebuf.at[p],
            dst_ref=fbuf.at[seq],
            send_sem=back_sem.at[0],
            recv_sem=back_sem.at[1],
            device_id=(p, head),
            device_id_type=MESH,
        ).start()
        return carry

    lax.fori_loop(1, n, send_back, 0)
    fbuf[seq] = ebuf[seq]

    within(1)
    load_g.wait()
    for j in range(PAIRS):
        sg[j] = gate(0.5 * gb[:, j * 128 : (j + 1) * 128].astype(F32))

    wait_all(back_sem.at[0], fbuf.at[pl.ds(0, n - 1)])
    wait_all(back_sem.at[1], fbuf.at[pl.ds(0, n - 1)])

    squares = jnp.zeros((TOK, 128), F32)
    for j in range(PAIRS):
        y = yv[j]
        for s in range(2):
            pieces = []
            for i in range(8):
                t = s * 32 + i * PAIRS + j
                pieces.append(fbuf[t // tp, t % tp])
            entering = jnp.concatenate(pieces, axis=0)
            c_all = jnp.concatenate([cv[s * 2, 1], cv[s * 2 + 1, 1]], axis=0)
            y = y + infl[s, j] * mm(c_all, entering)
        mixed = y * sg[j]
        yv[j] = mixed
        squares = squares + mixed * mixed
    sums = jnp.concatenate(
        [
            jnp.sum(jnp.transpose(squares[b * 128 : (b + 1) * 128]), axis=0, keepdims=True)
            for b in range(2)
        ],
        axis=1,
    )
    hbuf[head] = sums

    def send_sums(d, carry):
        p = lax.rem(head + d, nh)
        pltpu.make_async_remote_copy(
            src_ref=hbuf.at[head],
            dst_ref=hbuf.at[head],
            send_sem=head_sem.at[0],
            recv_sem=head_sem.at[1],
            device_id=(seq, p),
            device_id_type=MESH,
        ).start()
        return carry

    lax.fori_loop(1, nh, send_sums, 0)
    wait_all(head_sem.at[0], hbuf.at[pl.ds(0, nh - 1)])
    wait_all(head_sem.at[1], hbuf.at[pl.ds(0, nh - 1)])
    load_gain.wait()
    total = hbuf[0]
    for p in range(1, nh):
        total = total + hbuf[p]
    scale = lax.rsqrt(total * (1.0 / channels) + 1e-5)
    for b in range(2):
        column = jnp.transpose(jnp.broadcast_to(scale[:, b * 128 : (b + 1) * 128], (128, 128)))
        for j in range(PAIRS):
            lanes = slice(j * 128, (j + 1) * 128)
            ob[b * 128 : (b + 1) * 128, lanes] = (
                yv[j, b * 128 : (b + 1) * 128] * column * gain[:, lanes]
            ).astype(BF16)
    store = pltpu.make_async_copy(ob, out_hbm, out_sem)
    store.start()
    store.wait()


def body(
    inputs,
    gating,
    state_proj,
    conv_inputs,
    conv_state,
    step_raw,
    step_bias,
    decay_log,
    skip_gain,
    norm_gain,
    boundaries,
):
    n = lax.axis_size("seq")
    nh = lax.axis_size("head")
    tp = TILES // n
    fj = 1 if tp == 1 else PAIRS
    width = inputs.shape[1]
    hbm = pl.BlockSpec(memory_space=pl.ANY)
    smem = pl.BlockSpec(memory_space=pltpu.SMEM)
    vm = pltpu.VMEM
    dma = pltpu.SemaphoreType.DMA
    return pl.pallas_call(
        functools.partial(kernel, n, nh, width * nh),
        out_shape=jax.ShapeDtypeStruct(inputs.shape, BF16),
        in_specs=[hbm] * 7 + [smem] * 4,
        out_specs=hbm,
        scratch_shapes=[
            vm((TOK, 512), BF16),
            vm((TOK, 512), BF16),
            vm((TOK, 256), BF16),
            vm((4, 512), F32),
            vm((4, 256), F32),
            vm((8, TOK), BF16),
            vm((1, 512), F32),
            vm((16, 512), BF16),
            vm((16, 512), BF16),
            vm((16, 256), BF16),
            vm((16, 256), BF16),
            vm((TOK + 2 * PAD, 512), F32),
            vm((TOK + 2 * PAD, 256), F32),
            vm((4, PAIRS, 256, 128), BF16),
            vm((4, 2, 128, 128), BF16),
            vm((4, 128, 128), F32),
            vm((4, 128, 128), F32),
            vm((4, 128, 128), F32),
            vm((4, 128, 128), F32),
            vm((2, PAIRS, 128, 128), BF16),
            vm((PAIRS, TOK, 128), F32),
            vm((2, PAIRS, TOK, 128), F32),
            vm((PAIRS, TOK, 128), F32),
            vm((2 * PAIRS, 1, 128), F32),
            vm((n, fj, 1, 128), F32),
            vm((n, tp, 16, 128), BF16),
            vm((n, tp, 16, 128), BF16),
            vm((n, tp, 16, 128), BF16),
            vm((n, tp, 16, 128), BF16),
            vm((nh, 1, TOK), F32),
            vm((TOK, 512), BF16),
            dma((7,)),
            dma,
            dma((4,)),
            dma((4,)),
            dma((2,)),
            dma((2,)),
            dma((2,)),
            dma((2,)),
        ],
        compiler_params=pltpu.CompilerParams(
            collective_id=0, has_side_effects=True, vmem_limit_bytes=32 * 1024 * 1024
        ),
        cost_estimate=pl.CostEstimate(
            flops=400_000_000, bytes_accessed=1_000_000, transcendentals=1_000_000
        ),
    )(
        inputs,
        gating,
        state_proj,
        conv_inputs,
        conv_state,
        step_raw,
        norm_gain.reshape(1, width),
        step_bias,
        decay_log,
        skip_gain,
        boundaries,
    )


def solution(mesh):
    placed = (
        P("seq", "head"),
        P("seq", "head"),
        P("seq", None),
        P(None, "head"),
        P(),
        P("head", "seq"),
        P("head"),
        P("head"),
        P("head"),
        P("head"),
        P(),
    )
    return jax.shard_map(
        body, mesh=mesh, in_specs=placed, out_specs=P("seq", "head"), check_vma=False
    )
```

```python
import functools

import jax
import jax.numpy as jnp
from jax import lax
from jax.experimental import pallas as pl
from jax.experimental.pallas import tpu as pltpu
from jax.sharding import PartitionSpec as P

MESH = pl.DeviceIdType.MESH
LOG2E = 1.4426950408889634
NEG = -1e30
F32 = jnp.float32
BF16 = jnp.bfloat16
TOK = 256
GROUP = 128
PAIRS = 4
TILES = 64
PAD = 8


def mm(a, b):
    return lax.dot_general(a, b, (((1,), (0,)), ((), ())), preferred_element_type=F32)


def mm_nt(a, b):
    return lax.dot_general(a, b, (((1,), (1,)), ((), ())), preferred_element_type=F32)


def mm_exact(a, b):
    return lax.dot_general(
        a, b, (((1,), (0,)), ((), ())), preferred_element_type=F32, precision=lax.Precision.HIGHEST
    )


def gate(half):
    return half + half * jnp.tanh(half)


def kernel(
    n,
    nh,
    channels,
    x_hbm,
    g_hbm,
    s_hbm,
    cx_hbm,
    cs_hbm,
    raw_hbm,
    gain_hbm,
    bias_hbm,
    dlog_hbm,
    skip_hbm,
    bounds_hbm,
    out_hbm,
    bias,
    dlog,
    skip,
    bounds,
    xb,
    gb,
    sb,
    cx,
    cs,
    raw,
    gain,
    xl,
    xr,
    sl,
    sr,
    xp,
    sp,
    xd,
    cv,
    bt,
    late,
    gm,
    mk,
    kp,
    st,
    yv,
    infl,
    sg,
    dsend,
    drecv,
    sbuf,
    rbuf,
    ebuf,
    fbuf,
    hbuf,
    ob,
    in_sem,
    out_sem,
    halo_send,
    halo_recv,
    fac_sem,
    tile_sem,
    back_sem,
    head_sem,
    near_sem,
    mate_sem,
):
    seq = lax.axis_index("seq")
    head = lax.axis_index("head")
    tp = TILES // n
    fj = 1 if tp == 1 else PAIRS

    def load(i, src, dst):
        copy = pltpu.make_async_copy(src, dst, in_sem.at[i])
        copy.start()
        return copy

    load_bias = load(7, bias_hbm, bias)
    load_dlog = load(8, dlog_hbm, dlog)
    load_bounds = load(9, bounds_hbm, bounds)
    load_skip = load(10, skip_hbm, skip)
    load_raw = load(0, raw_hbm, raw)
    load_s = load(1, s_hbm, sb)
    load_cs = load(2, cs_hbm, cs)
    load_x = load(3, x_hbm, xb)
    load_cx = load(4, cx_hbm, cx)
    load_g = load(5, g_hbm, gb)
    load_gain = load(6, gain_hbm, gain)

    lines = n // 4
    line = seq // 4
    place = lax.rem(seq, 4)
    across = (
        3 - place,
        lax.rem(place + 2, 4),
        place + 1 - 2 * lax.rem(place, 2),
        place,
    )

    def to_peers(act):
        for at in across:
            first = 1 if at is place else 0

            def one(d, carry):
                act(lax.rem(line + d, lines) * 4 + at)
                return carry

            lax.fori_loop(first, lines, one, 0)

    core = lax.rem(head, 2)
    ring = nh // 2
    mate = head + 1 - 2 * core
    up = lax.rem(head + 2, nh)
    down = lax.rem(head + nh - 2, nh)
    beside = (up, down) if ring > 2 else ((up,) if ring == 2 else ())

    barrier = pltpu.get_barrier_semaphore()
    to_peers(
        lambda p: pl.semaphore_signal(barrier, inc=1, device_id=(p, head), device_id_type=MESH)
    )
    for other in (mate,) + beside:
        pl.semaphore_signal(barrier, inc=1, device_id=(seq, other), device_id_type=MESH)

    load_raw.wait()
    load_bias.wait()
    load_dlog.wait()
    sub = lax.broadcasted_iota(jnp.int32, (8, 128), 0)
    lane = lax.broadcasted_iota(jnp.int32, (1, 128), 1)
    left = lane < 64
    bias_col = jnp.zeros((8, 128), F32)
    rate_col = jnp.zeros((8, 128), F32)
    for h in range(8):
        bias_col = jnp.where(sub == h, bias[h], bias_col)
        rate_col = jnp.where(sub == h, dlog[h], rate_col)
    rate_col = -LOG2E * jnp.exp(rate_col)
    steps = []
    for b in range(2):
        z = raw[:, b * 128 : (b + 1) * 128].astype(F32) + bias_col
        small = jnp.exp(-jnp.abs(z))
        one = 1.0 + small
        exact = jnp.where(one == 1.0, small, jnp.log(one) * (small / jnp.where(one == 1.0, 1.0, one - 1.0)))
        steps.append(jnp.maximum(z, 0.0) + exact)
    decay = jnp.concatenate([steps[0] * rate_col, steps[1] * rate_col], axis=0)
    log_step = jnp.log(jnp.concatenate(steps, axis=0)) * LOG2E
    row_i = lax.broadcasted_iota(jnp.int32, (128, 128), 0)
    col_i = lax.broadcasted_iota(jnp.int32, (128, 128), 1)
    cum_f = mm_exact(decay, (row_i <= col_i).astype(F32))
    cum_b = mm_exact(decay, (row_i >= col_i).astype(F32))
    cums = (cum_f, cum_b)
    cols = jnp.transpose(jnp.concatenate([cum_f, cum_b, jnp.zeros((96, 128), F32)], axis=0))
    minus = (cum_f - log_step, cum_b - log_step)

    load_bounds.wait()
    base = seq * TOK

    def label(position):
        count = jnp.zeros_like(position)
        for i in range(8):
            count = count + (bounds[i] <= position).astype(jnp.int32)
        return count

    first = (label(base), label(base + 128))
    last = (label(base + 127), label(base + 255))
    prev = (label(base - 1), last[0])
    after = (first[1], label(base + 256))
    rows_of = [None, None]
    ends = []
    passes = []
    tails = []
    for s in range(2):
        ends.append([])
        passes.append([])
        tails.append([])
        for b in range(2):
            block = cums[s][b * 8 : (b + 1) * 8]
            end = jnp.broadcast_to(block[:, 127:128] if s == 0 else block[:, 0:1], (8, 128))
            ends[s].append(end)
            end_label = last[b] if s == 0 else first[b]
            outside = prev[b] if s == 0 else after[b]
            passes[s].append(jnp.where(end_label == outside, jnp.exp2(end), 0.0))
            labels = label(base + b * 128 + lax.broadcasted_iota(jnp.int32, (8, 128), 1))
            tails[s].append(
                jnp.where(
                    labels == end_label, jnp.exp2(end - minus[s][b * 8 : (b + 1) * 8]), 0.0
                )
            )
            rows_of[b] = labels[0:1]

    def spread(column, j):
        return jnp.where(left, column[2 * j : 2 * j + 1], column[2 * j + 1 : 2 * j + 2])

    for s in range(2):
        factor = passes[s][0] * passes[s][1]
        for j in range(PAIRS):
            dsend[s * PAIRS + j] = spread(factor, j)

    load_s.wait()
    load_cs.wait()
    load_x.wait()
    load_cx.wait()

    xp[PAD : PAD + TOK] = xb[...].astype(F32)
    sp[PAD : PAD + TOK] = sb[...].astype(F32)

    def conv(padded, taps, c, r0, rows, s):
        lanes = slice(c * 128, (c + 1) * 128)
        total = None
        for k in range(4):
            shift = -k if s == 0 else k
            term = (0.5 * taps[k : k + 1, lanes]) * padded[
                PAD + r0 + shift : PAD + r0 + shift + rows, lanes
            ]
            total = term if total is None else total + term
        return gate(total)

    def conv_x(j, r0, rows, s):
        v = conv(xp, cx, j, r0, rows, s)
        b = r0 // 128
        r = r0 - b * 128
        xd[s * 2 + b, j, r : r + rows] = jnp.where(left, v, 0.0).astype(BF16)
        xd[s * 2 + b, j, 128 + r : 128 + r + rows] = jnp.where(left, 0.0, v).astype(BF16)

    def conv_s(c, r0, rows, s):
        v = conv(sp, cs, c, r0, rows, s)
        b = r0 // 128
        r = r0 - b * 128
        cv[s * 2 + b, c, r : r + rows] = v.astype(BF16)

    inner = (
        (0, ((16, 48), (64, 64), (128, 64), (192, 64))),
        (1, ((0, 64), (64, 64), (128, 64), (192, 48))),
    )
    edges = ((0, 0), (1, TOK - 16))
    for c in range(2):
        for s, chunks in inner:
            for r0, rows in chunks:
                conv_s(c, r0, rows, s)
    for j in range(PAIRS):
        for s, chunks in inner:
            for r0, rows in chunks:
                conv_x(j, r0, rows, s)

    def block_state(s, b, j):
        q = s * 2 + b
        scaled = jnp.concatenate(
            [bt[q] * tails[s][b][2 * j + k : 2 * j + k + 1] for k in range(2)], axis=1
        ).astype(BF16)
        return mm(scaled, xd[q, j])

    for s in range(2):
        bt[s * 2 + 1 - s] = jnp.transpose(cv[s * 2 + 1 - s, 0].astype(F32))
        for j in range(PAIRS):
            late[s, j] = block_state(s, 1 - s, j)

    pl.semaphore_wait(barrier, n - 1 + 1 + len(beside))

    right_dev = (lax.rem(seq + 1, n), head)
    left_dev = (lax.rem(seq + n - 1, n), head)
    halos = []
    for i, (src, dst, dev) in enumerate(
        (
            (x_hbm.at[TOK - 16 : TOK], xl, right_dev),
            (s_hbm.at[TOK - 16 : TOK], sl, right_dev),
            (x_hbm.at[0:16], xr, left_dev),
            (s_hbm.at[0:16], sr, left_dev),
        )
    ):
        copy = pltpu.make_async_remote_copy(
            src_ref=src,
            dst_ref=dst,
            send_sem=halo_send.at[i],
            recv_sem=halo_recv.at[i],
            device_id=dev,
            device_id_type=MESH,
        )
        copy.start()
        halos.append(copy)

    def send_factor(p):
        tile = p * tp
        strand = tile // 32
        at = strand * PAIRS + (lax.rem(tile, PAIRS) if fj == 1 else 0)
        pltpu.make_async_remote_copy(
            src_ref=dsend.at[pl.ds(at, fj)],
            dst_ref=drecv.at[seq],
            send_sem=fac_sem.at[0],
            recv_sem=fac_sem.at[1],
            device_id=(p, head),
            device_id_type=MESH,
        ).start()

    to_peers(send_factor)
    for other in beside:
        pl.semaphore_signal(near_sem, inc=1, device_id=(seq, other), device_id_type=MESH)
    tile0 = seq * tp
    at0 = (tile0 // 32) * PAIRS + (lax.rem(tile0, PAIRS) if fj == 1 else 0)
    drecv[seq] = dsend[pl.ds(at0, fj)]

    for s in range(2):
        for b in range(2):
            outside = prev[b] if s == 0 else after[b]
            tok = label(base + b * 128 + row_i)
            order = row_i >= col_i if s == 0 else row_i <= col_i
            mk[s * 2 + b] = jnp.where((tok == rows_of[b]) & order, 0.0, NEG)
            kp[s * 2 + b] = jnp.where(tok == outside, 0.0, NEG)
    load_g.wait()
    for j in range(PAIRS):
        sg[j] = gate(0.5 * gb[:, j * 128 : (j + 1) * 128].astype(F32))

    for copy in halos:
        copy.wait_recv()
    has_left = seq > 0
    has_right = seq < n - 1
    xp[0:PAD] = jnp.where(has_left, xl[...].astype(F32)[16 - PAD :], 0.0)
    xp[PAD + TOK : PAD + TOK + PAD] = jnp.where(has_right, xr[...].astype(F32)[:PAD], 0.0)
    sp[0:PAD] = jnp.where(has_left, sl[...].astype(F32)[16 - PAD :], 0.0)
    sp[PAD + TOK : PAD + TOK + PAD] = jnp.where(has_right, sr[...].astype(F32)[:PAD], 0.0)
    for s, r0 in edges:
        for c in range(2):
            conv_s(c, r0, 16, s)
        for j in range(PAIRS):
            conv_x(j, r0, 16, s)

    for s in range(2):
        bt[s * 3] = jnp.transpose(cv[s * 3, 0].astype(F32))
    for j in range(PAIRS):
        for s in range(2):
            early = block_state(s, s, j)
            st[s, j] = early.astype(BF16)
            total = (spread(passes[s][1 - s], j) * early + late[s, j]).astype(BF16)
            for i in range(8):
                t = s * 32 + i * PAIRS + j
                sbuf[t // tp, t % tp] = total[i * 16 : (i + 1) * 16]

    def send_tile(p):
        pltpu.make_async_remote_copy(
            src_ref=sbuf.at[p],
            dst_ref=rbuf.at[seq],
            send_sem=tile_sem.at[0],
            recv_sem=tile_sem.at[1],
            device_id=(p, head),
            device_id_type=MESH,
        ).start()

    to_peers(send_tile)
    rbuf[seq] = sbuf[seq]

    if beside:
        pl.semaphore_wait(near_sem, len(beside))
        pl.semaphore_signal(mate_sem, inc=1, device_id=(seq, mate), device_id_type=MESH)

    def within(b):
        if b == 0:
            for q in range(4):
                gm[q] = mm_nt(cv[q, 1], cv[q, 0])
        for j in range(PAIRS):
            total = None
            for s in range(2):
                q = s * 2 + b
                wide = []
                parts = []
                for k in range(2):
                    h = 2 * j + k
                    at = s * 16 + b * 8 + h
                    column = jnp.broadcast_to(cols[:, at : at + 1], (128, 128))
                    wide.append(column)
                    row = minus[s][b * 8 + h : b * 8 + h + 1]
                    parts.append((jnp.exp2(column - row + mk[q]) * gm[q]).astype(BF16))
                values = xd[q, j]
                term = mm(jnp.concatenate(parts, axis=1), values)
                sk = jnp.where(left, skip[2 * j], skip[2 * j + 1])
                term = term + sk * (values[:128].astype(F32) + values[128:].astype(F32))
                flow = jnp.exp2(jnp.where(left, wide[0], wide[1]) + kp[q])
                if b != s:
                    term = term + flow * mm(cv[q, 1], st[s, j])
                    flow = flow * spread(passes[s][s], j)
                infl[s, j, b * 128 : (b + 1) * 128] = flow
                total = term if total is None else total + term
            yv[j, b * 128 : (b + 1) * 128] = total

    load_skip.wait()
    within(0)
    within(1)

    def wait_all(sem, ref):
        pltpu.make_async_copy(ref, ref, sem).wait()

    wait_all(fac_sem.at[1], drecv.at[pl.ds(0, n - 1)])
    wait_all(tile_sem.at[1], rbuf.at[pl.ds(0, n - 1)])

    reverse = tile0 >= 32

    def scan(i, carry):
        k = jnp.where(reverse, n - 1 - i, i)
        new = []
        for t in range(tp):
            ebuf[k, t] = carry[t].astype(BF16)
            new.append(drecv[k, t % fj] * carry[t] + rbuf[k, t].astype(F32))
        return tuple(new)

    lax.fori_loop(
        0, n, scan, tuple(jnp.zeros((16, 128), F32) for _ in range(tp)), unroll=4
    )

    def send_back(p):
        pltpu.make_async_remote_copy(
            src_ref=ebuf.at[p],
            dst_ref=fbuf.at[seq],
            send_sem=back_sem.at[0],
            recv_sem=back_sem.at[1],
            device_id=(p, head),
            device_id_type=MESH,
        ).start()

    to_peers(send_back)
    fbuf[seq] = ebuf[seq]
    load_gain.wait()
    wait_all(back_sem.at[1], fbuf.at[pl.ds(0, n - 1)])

    squares = jnp.zeros((TOK, 128), F32)
    for j in range(PAIRS):
        y = yv[j]
        for s in range(2):
            pieces = []
            for i in range(8):
                t = s * 32 + i * PAIRS + j
                pieces.append(fbuf[t // tp, t % tp])
            entering = jnp.concatenate(pieces, axis=0)
            c_all = jnp.concatenate([cv[s * 2, 1], cv[s * 2 + 1, 1]], axis=0)
            y = y + infl[s, j] * mm(c_all, entering)
        mixed = y * sg[j]
        yv[j] = mixed * gain[:, j * 128 : (j + 1) * 128]
        squares = squares + mixed * mixed
    sums = jnp.concatenate(
        [
            jnp.sum(jnp.transpose(squares[b * 128 : (b + 1) * 128]), axis=0, keepdims=True)
            for b in range(2)
        ],
        axis=1,
    )
    hbuf[head] = sums

    def send_sums(d, carry):
        p = lax.rem(head + d, nh)
        pltpu.make_async_remote_copy(
            src_ref=hbuf.at[head],
            dst_ref=hbuf.at[head],
            send_sem=head_sem.at[0],
            recv_sem=head_sem.at[1],
            device_id=(seq, p),
            device_id_type=MESH,
        ).start()
        return carry

    if beside:
        pl.semaphore_wait(mate_sem, 1)
    lax.fori_loop(1, nh, send_sums, 0)
    wait_all(head_sem.at[1], hbuf.at[pl.ds(0, nh - 1)])
    total = hbuf[0]
    for p in range(1, nh):
        total = total + hbuf[p]
    scale = lax.rsqrt(total * (1.0 / channels) + 1e-5)
    for b in range(2):
        column = jnp.transpose(jnp.broadcast_to(scale[:, b * 128 : (b + 1) * 128], (128, 128)))
        for j in range(PAIRS):
            lanes = slice(j * 128, (j + 1) * 128)
            ob[b * 128 : (b + 1) * 128, lanes] = (
                yv[j, b * 128 : (b + 1) * 128] * column
            ).astype(BF16)
    store = pltpu.make_async_copy(ob, out_hbm, out_sem)
    store.start()
    for copy in halos:
        copy.wait_send()
    wait_all(fac_sem.at[0], drecv.at[pl.ds(0, n - 1)])
    wait_all(tile_sem.at[0], rbuf.at[pl.ds(0, n - 1)])
    wait_all(back_sem.at[0], fbuf.at[pl.ds(0, n - 1)])
    wait_all(head_sem.at[0], hbuf.at[pl.ds(0, nh - 1)])
    store.wait()


def body(
    inputs,
    gating,
    state_proj,
    conv_inputs,
    conv_state,
    step_raw,
    step_bias,
    decay_log,
    skip_gain,
    norm_gain,
    boundaries,
):
    n = lax.axis_size("seq")
    nh = lax.axis_size("head")
    tp = TILES // n
    fj = 1 if tp == 1 else PAIRS
    width = inputs.shape[1]
    hbm = pl.BlockSpec(memory_space=pltpu.HBM)
    smem = pltpu.SMEM
    vm = pltpu.VMEM
    dma = pltpu.SemaphoreType.DMA
    return pl.pallas_call(
        functools.partial(kernel, n, nh, width * nh),
        out_shape=jax.ShapeDtypeStruct(inputs.shape, BF16),
        in_specs=[hbm] * 11,
        out_specs=hbm,
        scratch_shapes=[
            smem((8,), F32),
            smem((8,), F32),
            smem((8,), F32),
            smem((8,), jnp.int32),
            vm((TOK, 512), BF16),
            vm((TOK, 512), BF16),
            vm((TOK, 256), BF16),
            vm((4, 512), F32),
            vm((4, 256), F32),
            vm((8, TOK), BF16),
            vm((1, 512), F32),
            vm((16, 512), BF16),
            vm((16, 512), BF16),
            vm((16, 256), BF16),
            vm((16, 256), BF16),
            vm((TOK + 2 * PAD, 512), F32),
            vm((TOK + 2 * PAD, 256), F32),
            vm((4, PAIRS, 256, 128), BF16),
            vm((4, 2, 128, 128), BF16),
            vm((4, 128, 128), F32),
            vm((2, PAIRS, 128, 128), F32),
            vm((4, 128, 128), F32),
            vm((4, 128, 128), F32),
            vm((4, 128, 128), F32),
            vm((2, PAIRS, 128, 128), BF16),
            vm((PAIRS, TOK, 128), F32),
            vm((2, PAIRS, TOK, 128), F32),
            vm((PAIRS, TOK, 128), F32),
            vm((2 * PAIRS, 1, 128), F32),
            vm((n, fj, 1, 128), F32),
            vm((n, tp, 16, 128), BF16),
            vm((n, tp, 16, 128), BF16),
            vm((n, tp, 16, 128), BF16),
            vm((n, tp, 16, 128), BF16),
            vm((nh, 1, TOK), F32),
            vm((TOK, 512), BF16),
            dma((11,)),
            dma,
            dma((4,)),
            dma((4,)),
            dma((2,)),
            dma((2,)),
            dma((2,)),
            dma((2,)),
            pltpu.SemaphoreType.REGULAR,
            pltpu.SemaphoreType.REGULAR,
        ],
        compiler_params=pltpu.CompilerParams(
            collective_id=0, has_side_effects=True, vmem_limit_bytes=56 * 1024 * 1024
        ),
        cost_estimate=pl.CostEstimate(
            flops=400_000_000, bytes_accessed=1_000_000, transcendentals=1_000_000
        ),
    )(
        inputs,
        gating,
        state_proj,
        conv_inputs,
        conv_state,
        step_raw,
        norm_gain.reshape(1, width),
        step_bias,
        decay_log,
        skip_gain,
        boundaries,
    )


def solution(mesh):
    placed = (
        P("seq", "head"),
        P("seq", "head"),
        P("seq", None),
        P(None, "head"),
        P(),
        P("head", "seq"),
        P("head"),
        P("head"),
        P("head"),
        P("head"),
        P(),
    )
    return jax.shard_map(
        body, mesh=mesh, in_specs=placed, out_specs=P("seq", "head"), check_vma=False
    )
```

```python
import functools

import jax
import jax.numpy as jnp
from jax import lax
from jax.experimental import pallas as pl
from jax.experimental.pallas import tpu as pltpu
from jax.sharding import PartitionSpec as P

MESH = pl.DeviceIdType.MESH
LOG2E = 1.4426950408889634
NEG = -1e30
F32 = jnp.float32
BF16 = jnp.bfloat16
TOK = 256
GROUP = 128
PAIRS = 4
TILES = 64
PAD = 8


def mm(a, b):
    return lax.dot_general(a, b, (((1,), (0,)), ((), ())), preferred_element_type=F32)


def mm_nt(a, b):
    return lax.dot_general(a, b, (((1,), (1,)), ((), ())), preferred_element_type=F32)


def mm_exact(a, b):
    return lax.dot_general(
        a, b, (((1,), (0,)), ((), ())), preferred_element_type=F32, precision=lax.Precision.HIGHEST
    )


def gate(half):
    return half + half * jnp.tanh(half)


def kernel(
    n,
    nh,
    channels,
    x_hbm,
    g_hbm,
    s_hbm,
    cx_hbm,
    cs_hbm,
    raw_hbm,
    gain_hbm,
    bias_hbm,
    dlog_hbm,
    skip_hbm,
    bounds_hbm,
    out_hbm,
    bias,
    dlog,
    skip,
    bounds,
    xb,
    gb,
    sb,
    cx,
    cs,
    raw,
    gain,
    xl,
    xr,
    sl,
    sr,
    xp,
    sp,
    xd,
    cv,
    bt,
    late,
    gm,
    mk,
    kp,
    st,
    yv,
    infl,
    sg,
    dsend,
    drecv,
    sbuf,
    rbuf,
    ebuf,
    fbuf,
    hbuf,
    ob,
    in_sem,
    out_sem,
    halo_send,
    halo_recv,
    fac_sem,
    tile_sem,
    back_sem,
    head_sem,
    line_sem,
    near_sem,
    mate_sem,
):
    seq = lax.axis_index("seq")
    head = lax.axis_index("head")
    tp = TILES // n
    fj = 1 if tp == 1 else PAIRS

    def load(i, src, dst):
        copy = pltpu.make_async_copy(src, dst, in_sem.at[i])
        copy.start()
        return copy

    load_bias = load(7, bias_hbm, bias)
    load_dlog = load(8, dlog_hbm, dlog)
    load_bounds = load(9, bounds_hbm, bounds)
    load_skip = load(10, skip_hbm, skip)
    load_raw = load(0, raw_hbm, raw)
    load_s = load(1, s_hbm, sb)
    load_cs = load(2, cs_hbm, cs)
    load_x = load(3, x_hbm, xb)
    load_cx = load(4, cx_hbm, cx)
    load_g = load(5, g_hbm, gb)
    load_gain = load(6, gain_hbm, gain)

    lines = n // 4
    line = seq // 4
    place = lax.rem(seq, 4)
    across = (
        3 - place,
        lax.rem(place + 2, 4),
        place + 1 - 2 * lax.rem(place, 2),
        place,
    )

    def to_peers(act):
        for at in across:
            first = 1 if at is place else 0

            def one(d, carry):
                act(lax.rem(line + d, lines) * 4 + at)
                return carry

            lax.fori_loop(first, lines, one, 0, unroll=True)

    core = lax.rem(head, 2)
    ring = nh // 2
    mate = head + 1 - 2 * core
    up = lax.rem(head + 2, nh)
    down = lax.rem(head + nh - 2, nh)
    beside = (up, down) if ring > 2 else ((up,) if ring == 2 else ())

    barrier = pltpu.get_barrier_semaphore()
    right_dev = (lax.rem(seq + 1, n), head)
    left_dev = (lax.rem(seq + n - 1, n), head)
    greeted = [right_dev, left_dev]
    greeted += [(lax.rem(line + d, lines) * 4 + place, head) for d in range(1, lines)]
    greeted += [(line * 4 + at, head) for at in across[:3]]
    greeted += [(seq, other) for other in (mate,) + beside]
    for device in greeted:
        pl.semaphore_signal(barrier, inc=1, device_id=device, device_id_type=MESH)

    load_raw.wait()
    load_bias.wait()
    load_dlog.wait()
    sub = lax.broadcasted_iota(jnp.int32, (8, 128), 0)
    lane = lax.broadcasted_iota(jnp.int32, (1, 128), 1)
    left = lane < 64
    bias_col = jnp.zeros((8, 128), F32)
    rate_col = jnp.zeros((8, 128), F32)
    for h in range(8):
        bias_col = jnp.where(sub == h, bias[h], bias_col)
        rate_col = jnp.where(sub == h, dlog[h], rate_col)
    rate_col = -LOG2E * jnp.exp(rate_col)
    steps = []
    for b in range(2):
        z = raw[:, b * 128 : (b + 1) * 128].astype(F32) + bias_col
        small = jnp.exp(-jnp.abs(z))
        one = 1.0 + small
        exact = jnp.where(one == 1.0, small, jnp.log(one) * (small / jnp.where(one == 1.0, 1.0, one - 1.0)))
        steps.append(jnp.maximum(z, 0.0) + exact)
    decay = jnp.concatenate([steps[0] * rate_col, steps[1] * rate_col], axis=0)
    log_step = jnp.log(jnp.concatenate(steps, axis=0)) * LOG2E
    row_i = lax.broadcasted_iota(jnp.int32, (128, 128), 0)
    col_i = lax.broadcasted_iota(jnp.int32, (128, 128), 1)
    cum_f = mm_exact(decay, (row_i <= col_i).astype(F32))
    cum_b = mm_exact(decay, (row_i >= col_i).astype(F32))
    cums = (cum_f, cum_b)
    cols = jnp.transpose(jnp.concatenate([cum_f, cum_b, jnp.zeros((96, 128), F32)], axis=0))
    minus = (cum_f - log_step, cum_b - log_step)

    load_bounds.wait()
    base = seq * TOK

    def label(position):
        count = jnp.zeros_like(position)
        for i in range(8):
            count = count + (bounds[i] <= position).astype(jnp.int32)
        return count

    first = (label(base), label(base + 128))
    last = (label(base + 127), label(base + 255))
    prev = (label(base - 1), last[0])
    after = (first[1], label(base + 256))
    rows_of = [None, None]
    ends = []
    passes = []
    tails = []
    for s in range(2):
        ends.append([])
        passes.append([])
        tails.append([])
        for b in range(2):
            block = cums[s][b * 8 : (b + 1) * 8]
            end = jnp.broadcast_to(block[:, 127:128] if s == 0 else block[:, 0:1], (8, 128))
            ends[s].append(end)
            end_label = last[b] if s == 0 else first[b]
            outside = prev[b] if s == 0 else after[b]
            passes[s].append(jnp.where(end_label == outside, jnp.exp2(end), 0.0))
            labels = label(base + b * 128 + lax.broadcasted_iota(jnp.int32, (8, 128), 1))
            tails[s].append(
                jnp.where(
                    labels == end_label, jnp.exp2(end - minus[s][b * 8 : (b + 1) * 8]), 0.0
                )
            )
            rows_of[b] = labels[0:1]

    def spread(column, j):
        return jnp.where(left, column[2 * j : 2 * j + 1], column[2 * j + 1 : 2 * j + 2])

    for s in range(2):
        factor = passes[s][0] * passes[s][1]
        for j in range(PAIRS):
            dsend[s * PAIRS + j] = spread(factor, j)

    load_s.wait()
    load_cs.wait()
    load_x.wait()
    load_cx.wait()

    xp[PAD : PAD + TOK] = xb[...].astype(F32)
    sp[PAD : PAD + TOK] = sb[...].astype(F32)

    def conv(padded, taps, c, r0, rows, s):
        lanes = slice(c * 128, (c + 1) * 128)
        total = None
        for k in range(4):
            shift = -k if s == 0 else k
            term = (0.5 * taps[k : k + 1, lanes]) * padded[
                PAD + r0 + shift : PAD + r0 + shift + rows, lanes
            ]
            total = term if total is None else total + term
        return gate(total)

    def conv_x(j, r0, rows, s):
        v = conv(xp, cx, j, r0, rows, s)
        b = r0 // 128
        r = r0 - b * 128
        xd[s * 2 + b, j, r : r + rows] = jnp.where(left, v, 0.0).astype(BF16)
        xd[s * 2 + b, j, 128 + r : 128 + r + rows] = jnp.where(left, 0.0, v).astype(BF16)

    def conv_s(c, r0, rows, s):
        v = conv(sp, cs, c, r0, rows, s)
        b = r0 // 128
        r = r0 - b * 128
        cv[s * 2 + b, c, r : r + rows] = v.astype(BF16)

    inner = (
        (0, ((16, 48), (64, 64), (128, 64), (192, 64))),
        (1, ((0, 64), (64, 64), (128, 64), (192, 48))),
    )
    edges = ((0, 0), (1, TOK - 16))
    for c in range(2):
        for s, chunks in inner:
            for r0, rows in chunks:
                conv_s(c, r0, rows, s)
    for j in range(PAIRS):
        for s, chunks in inner:
            for r0, rows in chunks:
                conv_x(j, r0, rows, s)

    def block_state(s, b, j):
        q = s * 2 + b
        scaled = jnp.concatenate(
            [bt[q] * tails[s][b][2 * j + k : 2 * j + k + 1] for k in range(2)], axis=1
        ).astype(BF16)
        return mm(scaled, xd[q, j])

    for s in range(2):
        bt[s * 2 + 1 - s] = jnp.transpose(cv[s * 2 + 1 - s, 0].astype(F32))
        for j in range(PAIRS):
            late[s, j] = block_state(s, 1 - s, j)

    pl.semaphore_wait(barrier, len(greeted))

    halos = []
    for i, (src, dst, dev) in enumerate(
        (
            (x_hbm.at[TOK - 16 : TOK], xl, right_dev),
            (s_hbm.at[TOK - 16 : TOK], sl, right_dev),
            (x_hbm.at[0:16], xr, left_dev),
            (s_hbm.at[0:16], sr, left_dev),
        )
    ):
        copy = pltpu.make_async_remote_copy(
            src_ref=src,
            dst_ref=dst,
            send_sem=halo_send.at[i],
            recv_sem=halo_recv.at[i],
            device_id=dev,
            device_id_type=MESH,
        )
        copy.start()
        halos.append(copy)

    for at in across[:3]:
        pl.semaphore_signal(
            line_sem, inc=1, device_id=(line * 4 + at, head), device_id_type=MESH
        )
    for other in beside:
        pl.semaphore_signal(near_sem, inc=1, device_id=(seq, other), device_id_type=MESH)
    for s in range(2):
        for b in range(2):
            outside = prev[b] if s == 0 else after[b]
            tok = label(base + b * 128 + row_i)
            order = row_i >= col_i if s == 0 else row_i <= col_i
            mk[s * 2 + b] = jnp.where((tok == rows_of[b]) & order, 0.0, NEG)
            kp[s * 2 + b] = jnp.where(tok == outside, 0.0, NEG)
    load_g.wait()
    for j in range(PAIRS):
        sg[j] = gate(0.5 * gb[:, j * 128 : (j + 1) * 128].astype(F32))

    pl.semaphore_wait(line_sem, 3)

    def send_factor(p):
        tile = p * tp
        strand = tile // 32
        at = strand * PAIRS + (lax.rem(tile, PAIRS) if fj == 1 else 0)
        pltpu.make_async_remote_copy(
            src_ref=dsend.at[pl.ds(at, fj)],
            dst_ref=drecv.at[seq],
            send_sem=fac_sem.at[0],
            recv_sem=fac_sem.at[1],
            device_id=(p, head),
            device_id_type=MESH,
        ).start()

    to_peers(send_factor)
    tile0 = seq * tp
    at0 = (tile0 // 32) * PAIRS + (lax.rem(tile0, PAIRS) if fj == 1 else 0)
    drecv[seq] = dsend[pl.ds(at0, fj)]

    for copy in halos:
        copy.wait_recv()
    has_left = seq > 0
    has_right = seq < n - 1
    xp[0:PAD] = jnp.where(has_left, xl[...].astype(F32)[16 - PAD :], 0.0)
    xp[PAD + TOK : PAD + TOK + PAD] = jnp.where(has_right, xr[...].astype(F32)[:PAD], 0.0)
    sp[0:PAD] = jnp.where(has_left, sl[...].astype(F32)[16 - PAD :], 0.0)
    sp[PAD + TOK : PAD + TOK + PAD] = jnp.where(has_right, sr[...].astype(F32)[:PAD], 0.0)
    for s, r0 in edges:
        for c in range(2):
            conv_s(c, r0, 16, s)
        for j in range(PAIRS):
            conv_x(j, r0, 16, s)

    for s in range(2):
        bt[s * 3] = jnp.transpose(cv[s * 3, 0].astype(F32))
    for j in range(PAIRS):
        for s in range(2):
            early = block_state(s, s, j)
            st[s, j] = early.astype(BF16)
            total = (spread(passes[s][1 - s], j) * early + late[s, j]).astype(BF16)
            for i in range(8):
                t = s * 32 + i * PAIRS + j
                sbuf[t // tp, t % tp] = total[i * 16 : (i + 1) * 16]

    def send_tile(p):
        pltpu.make_async_remote_copy(
            src_ref=sbuf.at[p],
            dst_ref=rbuf.at[seq],
            send_sem=tile_sem.at[0],
            recv_sem=tile_sem.at[1],
            device_id=(p, head),
            device_id_type=MESH,
        ).start()

    to_peers(send_tile)
    rbuf[seq] = sbuf[seq]

    if beside:
        pl.semaphore_wait(near_sem, len(beside))
        pl.semaphore_signal(mate_sem, inc=1, device_id=(seq, mate), device_id_type=MESH)

    def within(b):
        if b == 0:
            for q in range(4):
                gm[q] = mm_nt(cv[q, 1], cv[q, 0])
        for j in range(PAIRS):
            total = None
            for s in range(2):
                q = s * 2 + b
                wide = []
                parts = []
                for k in range(2):
                    h = 2 * j + k
                    at = s * 16 + b * 8 + h
                    column = jnp.broadcast_to(cols[:, at : at + 1], (128, 128))
                    wide.append(column)
                    row = minus[s][b * 8 + h : b * 8 + h + 1]
                    parts.append((jnp.exp2(column - row + mk[q]) * gm[q]).astype(BF16))
                values = xd[q, j]
                term = mm(jnp.concatenate(parts, axis=1), values)
                sk = jnp.where(left, skip[2 * j], skip[2 * j + 1])
                term = term + sk * (values[:128].astype(F32) + values[128:].astype(F32))
                flow = jnp.exp2(jnp.where(left, wide[0], wide[1]) + kp[q])
                if b != s:
                    term = term + flow * mm(cv[q, 1], st[s, j])
                    flow = flow * spread(passes[s][s], j)
                infl[s, j, b * 128 : (b + 1) * 128] = flow
                total = term if total is None else total + term
            yv[j, b * 128 : (b + 1) * 128] = total

    load_skip.wait()
    within(0)
    within(1)

    def wait_all(sem, ref):
        pltpu.make_async_copy(ref, ref, sem).wait()

    wait_all(fac_sem.at[1], drecv.at[pl.ds(0, n - 1)])
    wait_all(tile_sem.at[1], rbuf.at[pl.ds(0, n - 1)])

    reverse = tile0 >= 32

    def scan(i, carry):
        k = jnp.where(reverse, n - 1 - i, i)
        new = []
        for t in range(tp):
            ebuf[k, t] = carry[t].astype(BF16)
            new.append(drecv[k, t % fj] * carry[t] + rbuf[k, t].astype(F32))
        return tuple(new)

    lax.fori_loop(
        0, n, scan, tuple(jnp.zeros((16, 128), F32) for _ in range(tp)), unroll=8
    )

    def send_back(p):
        pltpu.make_async_remote_copy(
            src_ref=ebuf.at[p],
            dst_ref=fbuf.at[seq],
            send_sem=back_sem.at[0],
            recv_sem=back_sem.at[1],
            device_id=(p, head),
            device_id_type=MESH,
        ).start()

    for at in range(4):

        def back_line(d, carry):
            p = lax.rem(line + d, lines) * 4 + at

            @pl.when(p != seq)
            def _():
                send_back(p)

            return carry

        lax.fori_loop(0, lines, back_line, 0, unroll=True)
    fbuf[seq] = ebuf[seq]
    load_gain.wait()
    wait_all(back_sem.at[1], fbuf.at[pl.ds(0, n - 1)])

    squares = jnp.zeros((TOK, 128), F32)
    for j in range(PAIRS):
        y = yv[j]
        for s in range(2):
            pieces = []
            for i in range(8):
                t = s * 32 + i * PAIRS + j
                pieces.append(fbuf[t // tp, t % tp])
            entering = jnp.concatenate(pieces, axis=0)
            c_all = jnp.concatenate([cv[s * 2, 1], cv[s * 2 + 1, 1]], axis=0)
            y = y + infl[s, j] * mm(c_all, entering)
        mixed = y * sg[j]
        yv[j] = mixed * gain[:, j * 128 : (j + 1) * 128]
        squares = squares + mixed * mixed
    sums = jnp.concatenate(
        [
            jnp.sum(jnp.transpose(squares[b * 128 : (b + 1) * 128]), axis=0, keepdims=True)
            for b in range(2)
        ],
        axis=1,
    )
    hbuf[head] = sums

    def send_sums(d, carry):
        p = lax.rem(head + d, nh)
        pltpu.make_async_remote_copy(
            src_ref=hbuf.at[head],
            dst_ref=hbuf.at[head],
            send_sem=head_sem.at[0],
            recv_sem=head_sem.at[1],
            device_id=(seq, p),
            device_id_type=MESH,
        ).start()
        return carry

    if beside:
        pl.semaphore_wait(mate_sem, 1)
    lax.fori_loop(1, nh, send_sums, 0)
    wait_all(head_sem.at[1], hbuf.at[pl.ds(0, nh - 1)])
    total = hbuf[0]
    for p in range(1, nh):
        total = total + hbuf[p]
    scale = lax.rsqrt(total * (1.0 / channels) + 1e-5)
    for b in range(2):
        column = jnp.transpose(jnp.broadcast_to(scale[:, b * 128 : (b + 1) * 128], (128, 128)))
        for j in range(PAIRS):
            lanes = slice(j * 128, (j + 1) * 128)
            out_hbm[b * 128 : (b + 1) * 128, lanes] = (
                yv[j, b * 128 : (b + 1) * 128] * column
            ).astype(BF16)
    for copy in halos:
        copy.wait_send()
    wait_all(fac_sem.at[0], drecv.at[pl.ds(0, n - 1)])
    wait_all(tile_sem.at[0], rbuf.at[pl.ds(0, n - 1)])
    wait_all(back_sem.at[0], fbuf.at[pl.ds(0, n - 1)])
    wait_all(head_sem.at[0], hbuf.at[pl.ds(0, nh - 1)])


def body(
    inputs,
    gating,
    state_proj,
    conv_inputs,
    conv_state,
    step_raw,
    step_bias,
    decay_log,
    skip_gain,
    norm_gain,
    boundaries,
):
    n = lax.axis_size("seq")
    nh = lax.axis_size("head")
    tp = TILES // n
    fj = 1 if tp == 1 else PAIRS
    width = inputs.shape[1]
    hbm = pl.BlockSpec(memory_space=pltpu.HBM)
    smem = pltpu.SMEM
    vm = pltpu.VMEM
    dma = pltpu.SemaphoreType.DMA
    return pl.pallas_call(
        functools.partial(kernel, n, nh, width * nh),
        out_shape=pltpu.VMEM(inputs.shape, BF16),
        in_specs=[hbm] * 11,
        out_specs=pl.BlockSpec(memory_space=pltpu.VMEM),
        scratch_shapes=[
            smem((8,), F32),
            smem((8,), F32),
            smem((8,), F32),
            smem((8,), jnp.int32),
            vm((TOK, 512), BF16),
            vm((TOK, 512), BF16),
            vm((TOK, 256), BF16),
            vm((4, 512), F32),
            vm((4, 256), F32),
            vm((8, TOK), BF16),
            vm((1, 512), F32),
            vm((16, 512), BF16),
            vm((16, 512), BF16),
            vm((16, 256), BF16),
            vm((16, 256), BF16),
            vm((TOK + 2 * PAD, 512), F32),
            vm((TOK + 2 * PAD, 256), F32),
            vm((4, PAIRS, 256, 128), BF16),
            vm((4, 2, 128, 128), BF16),
            vm((4, 128, 128), F32),
            vm((2, PAIRS, 128, 128), F32),
            vm((4, 128, 128), F32),
            vm((4, 128, 128), F32),
            vm((4, 128, 128), F32),
            vm((2, PAIRS, 128, 128), BF16),
            vm((PAIRS, TOK, 128), F32),
            vm((2, PAIRS, TOK, 128), F32),
            vm((PAIRS, TOK, 128), F32),
            vm((2 * PAIRS, 1, 128), F32),
            vm((n, fj, 1, 128), F32),
            vm((n, tp, 16, 128), BF16),
            vm((n, tp, 16, 128), BF16),
            vm((n, tp, 16, 128), BF16),
            vm((n, tp, 16, 128), BF16),
            vm((nh, 1, TOK), F32),
            vm((TOK, 512), BF16),
            dma((11,)),
            dma,
            dma((4,)),
            dma((4,)),
            dma((2,)),
            dma((2,)),
            dma((2,)),
            dma((2,)),
            pltpu.SemaphoreType.REGULAR,
            pltpu.SemaphoreType.REGULAR,
            pltpu.SemaphoreType.REGULAR,
        ],
        compiler_params=pltpu.CompilerParams(
            collective_id=0, has_side_effects=True, vmem_limit_bytes=56 * 1024 * 1024
        ),
        cost_estimate=pl.CostEstimate(
            flops=400_000_000, bytes_accessed=1_000_000, transcendentals=1_000_000
        ),
    )(
        inputs,
        gating,
        state_proj,
        conv_inputs,
        conv_state,
        step_raw,
        norm_gain.reshape(1, width),
        step_bias,
        decay_log,
        skip_gain,
        boundaries,
    )


def solution(mesh):
    placed = (
        P("seq", "head"),
        P("seq", "head"),
        P("seq", None),
        P(None, "head"),
        P(),
        P("head", "seq"),
        P("head"),
        P("head"),
        P("head"),
        P("head"),
        P(),
    )
    return jax.shard_map(
        body, mesh=mesh, in_specs=placed, out_specs=P("seq", "head"), check_vma=False
    )
```

```python
import functools

import jax
import jax.numpy as jnp
from jax import lax
from jax.experimental import pallas as pl
from jax.experimental.pallas import tpu as pltpu
from jax.sharding import PartitionSpec as P

MESH = pl.DeviceIdType.MESH
LOG2E = 1.4426950408889634
NEG = -1e30
F32 = jnp.float32
BF16 = jnp.bfloat16
TOK = 256
GROUP = 128
PAIRS = 4
TILES = 64
PAD = 8


def mm(a, b):
    return lax.dot_general(a, b, (((1,), (0,)), ((), ())), preferred_element_type=F32)


def mm_nt(a, b):
    return lax.dot_general(a, b, (((1,), (1,)), ((), ())), preferred_element_type=F32)


def mm_exact(a, b):
    return lax.dot_general(
        a, b, (((1,), (0,)), ((), ())), preferred_element_type=F32, precision=lax.Precision.HIGHEST
    )


def gate(half):
    return half + half * jnp.tanh(half)


def kernel(
    n,
    nh,
    channels,
    x_hbm,
    g_hbm,
    s_hbm,
    cx_hbm,
    cs_hbm,
    raw_hbm,
    gain_hbm,
    bias_hbm,
    dlog_hbm,
    skip_hbm,
    bounds_hbm,
    out_hbm,
    bias,
    dlog,
    skip,
    bounds,
    xb,
    gb,
    sb,
    cx,
    cs,
    raw,
    gain,
    edge,
    from_left,
    from_right,
    xp,
    sp,
    xd,
    cv,
    bt,
    late,
    gm,
    mk,
    kp,
    st,
    yv,
    infl,
    sg,
    dsend,
    drecv,
    sbuf,
    rbuf,
    ebuf,
    fbuf,
    hbuf,
    ob,
    in_sem,
    out_sem,
    halo_send,
    halo_recv,
    fac_sem,
    tile_sem,
    back_sem,
    head_sem,
    line_sem,
    near_sem,
    mate_sem,
):
    seq = lax.axis_index("seq")
    head = lax.axis_index("head")
    tp = TILES // n
    fj = 1 if tp == 1 else PAIRS

    def load(i, src, dst):
        copy = pltpu.make_async_copy(src, dst, in_sem.at[i])
        copy.start()
        return copy

    load_bias = load(7, bias_hbm, bias)
    load_dlog = load(8, dlog_hbm, dlog)
    load_bounds = load(9, bounds_hbm, bounds)
    load_skip = load(10, skip_hbm, skip)
    load_raw = load(0, raw_hbm, raw)
    load_s = load(1, s_hbm, sb)
    load_cs = load(2, cs_hbm, cs)
    load_x = load(3, x_hbm, xb)
    load_cx = load(4, cx_hbm, cx)
    load_g = load(5, g_hbm, gb)
    load_gain = load(6, gain_hbm, gain)

    lines = n // 4
    line = seq // 4
    place = lax.rem(seq, 4)
    across = (
        3 - place,
        lax.rem(place + 2, 4),
        place + 1 - 2 * lax.rem(place, 2),
        place,
    )

    def apart(d):
        return -min(d // 4, 4 - d // 4) - min(d % 4, 4 - d % 4)

    far_first = sorted(range(lines), key=apart)

    def to_peers(act):
        for at in across:
            for d in far_first:
                if at is not place or d > 0:
                    act(lax.rem(line + d, lines) * 4 + at)

    core = lax.rem(head, 2)
    ring = nh // 2
    mate = head + 1 - 2 * core
    up = lax.rem(head + 2, nh)
    down = lax.rem(head + nh - 2, nh)
    beside = (up, down) if ring > 2 else ((up,) if ring == 2 else ())

    barrier = pltpu.get_barrier_semaphore()
    right_dev = (lax.rem(seq + 1, n), head)
    left_dev = (lax.rem(seq + n - 1, n), head)
    greeted = [right_dev, left_dev]
    greeted += [(lax.rem(line + d, lines) * 4 + place, head) for d in range(1, lines)]
    greeted += [(line * 4 + at, head) for at in across[:3]]
    greeted += [(seq, other) for other in (mate,) + beside]
    for device in greeted:
        pl.semaphore_signal(barrier, inc=1, device_id=device, device_id_type=MESH)

    load_raw.wait()
    load_bias.wait()
    load_dlog.wait()
    sub = lax.broadcasted_iota(jnp.int32, (8, 128), 0)
    lane = lax.broadcasted_iota(jnp.int32, (1, 128), 1)
    left = lane < 64
    bias_col = jnp.zeros((8, 128), F32)
    rate_col = jnp.zeros((8, 128), F32)
    for h in range(8):
        bias_col = jnp.where(sub == h, bias[h], bias_col)
        rate_col = jnp.where(sub == h, dlog[h], rate_col)
    rate_col = -LOG2E * jnp.exp(rate_col)
    steps = []
    for b in range(2):
        z = raw[:, b * 128 : (b + 1) * 128].astype(F32) + bias_col
        small = jnp.exp(-jnp.abs(z))
        one = 1.0 + small
        exact = jnp.where(one == 1.0, small, jnp.log(one) * (small / jnp.where(one == 1.0, 1.0, one - 1.0)))
        steps.append(jnp.maximum(z, 0.0) + exact)
    decay = jnp.concatenate([steps[0] * rate_col, steps[1] * rate_col], axis=0)
    log_step = jnp.log(jnp.concatenate(steps, axis=0)) * LOG2E
    row_i = lax.broadcasted_iota(jnp.int32, (128, 128), 0)
    col_i = lax.broadcasted_iota(jnp.int32, (128, 128), 1)
    cum_f = mm_exact(decay, (row_i <= col_i).astype(F32))
    cum_b = mm_exact(decay, (row_i >= col_i).astype(F32))
    cums = (cum_f, cum_b)
    cols = jnp.transpose(jnp.concatenate([cum_f, cum_b, jnp.zeros((96, 128), F32)], axis=0))
    minus = (cum_f - log_step, cum_b - log_step)

    load_bounds.wait()
    base = seq * TOK

    def label(position):
        count = jnp.zeros_like(position)
        for i in range(8):
            count = count + (bounds[i] <= position).astype(jnp.int32)
        return count

    first = (label(base), label(base + 128))
    last = (label(base + 127), label(base + 255))
    prev = (label(base - 1), last[0])
    after = (first[1], label(base + 256))
    rows_of = [None, None]
    ends = []
    passes = []
    tails = []
    for s in range(2):
        ends.append([])
        passes.append([])
        tails.append([])
        for b in range(2):
            block = cums[s][b * 8 : (b + 1) * 8]
            end = jnp.broadcast_to(block[:, 127:128] if s == 0 else block[:, 0:1], (8, 128))
            ends[s].append(end)
            end_label = last[b] if s == 0 else first[b]
            outside = prev[b] if s == 0 else after[b]
            passes[s].append(jnp.where(end_label == outside, jnp.exp2(end), 0.0))
            labels = label(base + b * 128 + lax.broadcasted_iota(jnp.int32, (8, 128), 1))
            tails[s].append(
                jnp.where(
                    labels == end_label, jnp.exp2(end - minus[s][b * 8 : (b + 1) * 8]), 0.0
                )
            )
            rows_of[b] = labels[0:1]

    def spread(column, j):
        return jnp.where(left, column[2 * j : 2 * j + 1], column[2 * j + 1 : 2 * j + 2])

    for s in range(2):
        factor = passes[s][0] * passes[s][1]
        for j in range(PAIRS):
            dsend[s * PAIRS + j] = spread(factor, j)

    load_s.wait()
    load_cs.wait()
    load_x.wait()
    load_cx.wait()

    xp[PAD : PAD + TOK] = xb[...].astype(F32)
    sp[PAD : PAD + TOK] = sb[...].astype(F32)

    def conv(padded, taps, c, r0, rows, s):
        lanes = slice(c * 128, (c + 1) * 128)
        total = None
        for k in range(4):
            shift = -k if s == 0 else k
            term = (0.5 * taps[k : k + 1, lanes]) * padded[
                PAD + r0 + shift : PAD + r0 + shift + rows, lanes
            ]
            total = term if total is None else total + term
        return gate(total)

    def conv_x(j, r0, rows, s):
        v = conv(xp, cx, j, r0, rows, s)
        b = r0 // 128
        r = r0 - b * 128
        xd[s * 2 + b, j, r : r + rows] = jnp.where(left, v, 0.0).astype(BF16)
        xd[s * 2 + b, j, 128 + r : 128 + r + rows] = jnp.where(left, 0.0, v).astype(BF16)

    def conv_s(c, r0, rows, s):
        v = conv(sp, cs, c, r0, rows, s)
        b = r0 // 128
        r = r0 - b * 128
        cv[s * 2 + b, c, r : r + rows] = v.astype(BF16)

    inner = (
        (0, ((16, 48), (64, 64), (128, 64), (192, 64))),
        (1, ((0, 64), (64, 64), (128, 64), (192, 48))),
    )
    edges = ((0, 0), (1, TOK - 16))
    for c in range(2):
        for s, chunks in inner:
            for r0, rows in chunks:
                conv_s(c, r0, rows, s)
    for j in range(PAIRS):
        for s, chunks in inner:
            for r0, rows in chunks:
                conv_x(j, r0, rows, s)

    def block_state(s, b, j):
        q = s * 2 + b
        scaled = jnp.concatenate(
            [bt[q] * tails[s][b][2 * j + k : 2 * j + k + 1] for k in range(2)], axis=1
        ).astype(BF16)
        return mm(scaled, xd[q, j])

    for s in range(2):
        bt[s * 2 + 1 - s] = jnp.transpose(cv[s * 2 + 1 - s, 0].astype(F32))
        for j in range(PAIRS):
            late[s, j] = block_state(s, 1 - s, j)

    packed = ((xp, 0), (xp, 1), (xp, 2), (xp, 3), (sp, 0), (sp, 1))
    pad_row = jnp.zeros((1, 128), F32)
    for side, row in ((0, PAD + TOK - 3), (1, PAD)):
        rows = []
        for source, c in packed:
            rows += [source[row : row + 3, c * 128 : (c + 1) * 128], pad_row]
        rows.append(jnp.zeros((8, 128), F32))
        edge[side] = jnp.concatenate(rows, axis=0).astype(BF16)

    pl.semaphore_wait(barrier, len(greeted))

    halos = []
    for i, (src, dst, dev) in enumerate(
        ((edge.at[0], from_left, right_dev), (edge.at[1], from_right, left_dev))
    ):
        copy = pltpu.make_async_remote_copy(
            src_ref=src,
            dst_ref=dst,
            send_sem=halo_send.at[i],
            recv_sem=halo_recv.at[i],
            device_id=dev,
            device_id_type=MESH,
        )
        copy.start()
        halos.append(copy)

    for at in across[:3]:
        pl.semaphore_signal(
            line_sem, inc=1, device_id=(line * 4 + at, head), device_id_type=MESH
        )
    for other in beside:
        pl.semaphore_signal(near_sem, inc=1, device_id=(seq, other), device_id_type=MESH)
    for s in range(2):
        for b in range(2):
            outside = prev[b] if s == 0 else after[b]
            tok = label(base + b * 128 + row_i)
            order = row_i >= col_i if s == 0 else row_i <= col_i
            mk[s * 2 + b] = jnp.where((tok == rows_of[b]) & order, 0.0, NEG)
            kp[s * 2 + b] = jnp.where(tok == outside, 0.0, NEG)
    load_g.wait()
    for j in range(PAIRS):
        sg[j] = gate(0.5 * gb[:, j * 128 : (j + 1) * 128].astype(F32))

    pl.semaphore_wait(line_sem, 3)

    def send_factor(p):
        tile = p * tp
        strand = tile // 32
        at = strand * PAIRS + (lax.rem(tile, PAIRS) if fj == 1 else 0)
        pltpu.make_async_remote_copy(
            src_ref=dsend.at[pl.ds(at, fj)],
            dst_ref=drecv.at[seq],
            send_sem=fac_sem.at[0],
            recv_sem=fac_sem.at[1],
            device_id=(p, head),
            device_id_type=MESH,
        ).start()

    to_peers(send_factor)
    tile0 = seq * tp
    at0 = (tile0 // 32) * PAIRS + (lax.rem(tile0, PAIRS) if fj == 1 else 0)
    drecv[seq] = dsend[pl.ds(at0, fj)]

    for copy in halos:
        copy.wait_recv()
    has_left = seq > 0
    has_right = seq < n - 1
    for ref, row, inside in ((from_left, PAD - 3, has_left), (from_right, PAD + TOK, has_right)):
        values = jnp.where(inside, ref[...].astype(F32), 0.0)
        for at, (target, c) in enumerate(packed):
            target[row : row + 3, c * 128 : (c + 1) * 128] = values[4 * at : 4 * at + 3]
    for s, r0 in edges:
        for c in range(2):
            conv_s(c, r0, 16, s)
        for j in range(PAIRS):
            conv_x(j, r0, 16, s)

    for s in range(2):
        bt[s * 3] = jnp.transpose(cv[s * 3, 0].astype(F32))
    for j in range(PAIRS):
        for s in range(2):
            early = block_state(s, s, j)
            st[s, j] = early.astype(BF16)
            total = (spread(passes[s][1 - s], j) * early + late[s, j]).astype(BF16)
            for i in range(8):
                t = s * 32 + i * PAIRS + j
                sbuf[t // tp, t % tp] = total[i * 16 : (i + 1) * 16]

    def send_tile(p):
        pltpu.make_async_remote_copy(
            src_ref=sbuf.at[p],
            dst_ref=rbuf.at[seq],
            send_sem=tile_sem.at[0],
            recv_sem=tile_sem.at[1],
            device_id=(p, head),
            device_id_type=MESH,
        ).start()

    to_peers(send_tile)
    rbuf[seq] = sbuf[seq]

    if beside:
        pl.semaphore_wait(near_sem, len(beside))
        pl.semaphore_signal(mate_sem, inc=1, device_id=(seq, mate), device_id_type=MESH)

    def within(b):
        if b == 0:
            for q in range(4):
                gm[q] = mm_nt(cv[q, 1], cv[q, 0])
        for j in range(PAIRS):
            total = None
            for s in range(2):
                q = s * 2 + b
                wide = []
                parts = []
                for k in range(2):
                    h = 2 * j + k
                    at = s * 16 + b * 8 + h
                    column = jnp.broadcast_to(cols[:, at : at + 1], (128, 128))
                    wide.append(column)
                    row = minus[s][b * 8 + h : b * 8 + h + 1]
                    parts.append((jnp.exp2(column - row + mk[q]) * gm[q]).astype(BF16))
                values = xd[q, j]
                term = mm(jnp.concatenate(parts, axis=1), values)
                sk = jnp.where(left, skip[2 * j], skip[2 * j + 1])
                term = term + sk * (values[:128].astype(F32) + values[128:].astype(F32))
                flow = jnp.exp2(jnp.where(left, wide[0], wide[1]) + kp[q])
                if b != s:
                    term = term + flow * mm(cv[q, 1], st[s, j])
                    flow = flow * spread(passes[s][s], j)
                infl[s, j, b * 128 : (b + 1) * 128] = flow
                total = term if total is None else total + term
            yv[j, b * 128 : (b + 1) * 128] = total

    load_skip.wait()
    within(0)
    within(1)

    def wait_all(sem, ref):
        pltpu.make_async_copy(ref, ref, sem).wait()

    wait_all(fac_sem.at[1], drecv.at[pl.ds(0, n - 1)])
    wait_all(tile_sem.at[1], rbuf.at[pl.ds(0, n - 1)])

    reverse = tile0 >= 32

    def scan(i, carry):
        k = jnp.where(reverse, n - 1 - i, i)
        new = []
        for t in range(tp):
            ebuf[k, t] = carry[t].astype(BF16)
            new.append(drecv[k, t % fj] * carry[t] + rbuf[k, t].astype(F32))
        return tuple(new)

    lax.fori_loop(
        0, n, scan, tuple(jnp.zeros((16, 128), F32) for _ in range(tp)), unroll=8
    )

    def send_back(p):
        pltpu.make_async_remote_copy(
            src_ref=ebuf.at[p],
            dst_ref=fbuf.at[seq],
            send_sem=back_sem.at[0],
            recv_sem=back_sem.at[1],
            device_id=(p, head),
            device_id_type=MESH,
        ).start()

    def toward(p):
        @pl.when(p != seq)
        def _():
            send_back(p)

    for d in reversed(far_first):
        toward(d * 4)
    for at in range(1, 4):
        for d in far_first:
            toward(lax.rem(line + d, lines) * 4 + at)

    fbuf[seq] = ebuf[seq]
    load_gain.wait()
    wait_all(back_sem.at[1], fbuf.at[pl.ds(0, n - 1)])

    squares = jnp.zeros((TOK, 128), F32)
    for j in range(PAIRS):
        y = yv[j]
        for s in range(2):
            pieces = []
            for i in range(8):
                t = s * 32 + i * PAIRS + j
                pieces.append(fbuf[t // tp, t % tp])
            entering = jnp.concatenate(pieces, axis=0)
            c_all = jnp.concatenate([cv[s * 2, 1], cv[s * 2 + 1, 1]], axis=0)
            y = y + infl[s, j] * mm(c_all, entering)
        mixed = y * sg[j]
        yv[j] = mixed * gain[:, j * 128 : (j + 1) * 128]
        squares = squares + mixed * mixed
    sums = jnp.concatenate(
        [
            jnp.sum(jnp.transpose(squares[b * 128 : (b + 1) * 128]), axis=0, keepdims=True)
            for b in range(2)
        ],
        axis=1,
    )
    hbuf[head] = sums

    def send_sums(d, carry):
        p = lax.rem(head + d, nh)
        pltpu.make_async_remote_copy(
            src_ref=hbuf.at[head],
            dst_ref=hbuf.at[head],
            send_sem=head_sem.at[0],
            recv_sem=head_sem.at[1],
            device_id=(seq, p),
            device_id_type=MESH,
        ).start()
        return carry

    if beside:
        pl.semaphore_wait(mate_sem, 1)
    lax.fori_loop(1, nh, send_sums, 0)
    wait_all(head_sem.at[1], hbuf.at[pl.ds(0, nh - 1)])
    total = hbuf[0]
    for p in range(1, nh):
        total = total + hbuf[p]
    scale = lax.rsqrt(total * (1.0 / channels) + 1e-5)
    for b in range(2):
        column = jnp.transpose(jnp.broadcast_to(scale[:, b * 128 : (b + 1) * 128], (128, 128)))
        for j in range(PAIRS):
            lanes = slice(j * 128, (j + 1) * 128)
            out_hbm[b * 128 : (b + 1) * 128, lanes] = (
                yv[j, b * 128 : (b + 1) * 128] * column
            ).astype(BF16)
    for copy in halos:
        copy.wait_send()
    wait_all(fac_sem.at[0], drecv.at[pl.ds(0, n - 1)])
    wait_all(tile_sem.at[0], rbuf.at[pl.ds(0, n - 1)])
    wait_all(back_sem.at[0], fbuf.at[pl.ds(0, n - 1)])
    wait_all(head_sem.at[0], hbuf.at[pl.ds(0, nh - 1)])


def body(
    inputs,
    gating,
    state_proj,
    conv_inputs,
    conv_state,
    step_raw,
    step_bias,
    decay_log,
    skip_gain,
    norm_gain,
    boundaries,
):
    n = lax.axis_size("seq")
    nh = lax.axis_size("head")
    tp = TILES // n
    fj = 1 if tp == 1 else PAIRS
    width = inputs.shape[1]
    hbm = pl.BlockSpec(memory_space=pltpu.HBM)
    smem = pltpu.SMEM
    vm = pltpu.VMEM
    dma = pltpu.SemaphoreType.DMA
    return pl.pallas_call(
        functools.partial(kernel, n, nh, width * nh),
        out_shape=pltpu.VMEM(inputs.shape, BF16),
        in_specs=[hbm] * 11,
        out_specs=pl.BlockSpec(memory_space=pltpu.VMEM),
        scratch_shapes=[
            smem((8,), F32),
            smem((8,), F32),
            smem((8,), F32),
            smem((8,), jnp.int32),
            vm((TOK, 512), BF16),
            vm((TOK, 512), BF16),
            vm((TOK, 256), BF16),
            vm((4, 512), F32),
            vm((4, 256), F32),
            vm((8, TOK), BF16),
            vm((1, 512), F32),
            vm((2, 32, 128), BF16),
            vm((32, 128), BF16),
            vm((32, 128), BF16),
            vm((TOK + 2 * PAD, 512), F32),
            vm((TOK + 2 * PAD, 256), F32),
            vm((4, PAIRS, 256, 128), BF16),
            vm((4, 2, 128, 128), BF16),
            vm((4, 128, 128), F32),
            vm((2, PAIRS, 128, 128), F32),
            vm((4, 128, 128), F32),
            vm((4, 128, 128), F32),
            vm((4, 128, 128), F32),
            vm((2, PAIRS, 128, 128), BF16),
            vm((PAIRS, TOK, 128), F32),
            vm((2, PAIRS, TOK, 128), F32),
            vm((PAIRS, TOK, 128), F32),
            vm((2 * PAIRS, 1, 128), F32),
            vm((n, fj, 1, 128), F32),
            vm((n, tp, 16, 128), BF16),
            vm((n, tp, 16, 128), BF16),
            vm((n, tp, 16, 128), BF16),
            vm((n, tp, 16, 128), BF16),
            vm((nh, 1, TOK), F32),
            vm((TOK, 512), BF16),
            dma((11,)),
            dma,
            dma((4,)),
            dma((4,)),
            dma((2,)),
            dma((2,)),
            dma((2,)),
            dma((2,)),
            pltpu.SemaphoreType.REGULAR,
            pltpu.SemaphoreType.REGULAR,
            pltpu.SemaphoreType.REGULAR,
        ],
        compiler_params=pltpu.CompilerParams(
            collective_id=0, has_side_effects=True, vmem_limit_bytes=56 * 1024 * 1024
        ),
        cost_estimate=pl.CostEstimate(
            flops=400_000_000, bytes_accessed=1_000_000, transcendentals=1_000_000
        ),
    )(
        inputs,
        gating,
        state_proj,
        conv_inputs,
        conv_state,
        step_raw,
        norm_gain.reshape(1, width),
        step_bias,
        decay_log,
        skip_gain,
        boundaries,
    )


def solution(mesh):
    placed = (
        P("seq", "head"),
        P("seq", "head"),
        P("seq", None),
        P(None, "head"),
        P(),
        P("head", "seq"),
        P("head"),
        P("head"),
        P("head"),
        P("head"),
        P(),
    )
    return jax.shard_map(
        body, mesh=mesh, in_specs=placed, out_specs=P("seq", "head"), check_vma=False
    )
```

```python
import functools

import jax
import jax.numpy as jnp
from jax import lax
from jax.experimental import pallas as pl
from jax.experimental.pallas import tpu as pltpu
from jax.sharding import PartitionSpec as P

MESH = pl.DeviceIdType.MESH
LOG2E = 1.4426950408889634
NEG = -1e30
F32 = jnp.float32
BF16 = jnp.bfloat16
TOK = 256
GROUP = 128
PAIRS = 4
TILES = 64
PAD = 8


def mm(a, b):
    return lax.dot_general(a, b, (((1,), (0,)), ((), ())), preferred_element_type=F32)


def mm_nt(a, b):
    return lax.dot_general(a, b, (((1,), (1,)), ((), ())), preferred_element_type=F32)


def mm_exact(a, b):
    return lax.dot_general(
        a, b, (((1,), (0,)), ((), ())), preferred_element_type=F32, precision=lax.Precision.HIGHEST
    )


def gate(half):
    return half + half * jnp.tanh(half)


def kernel(
    n,
    nh,
    channels,
    x_hbm,
    g_hbm,
    s_hbm,
    cx_hbm,
    cs_hbm,
    raw_hbm,
    gain_hbm,
    bias_hbm,
    dlog_hbm,
    skip_hbm,
    bounds_hbm,
    out_hbm,
    bias,
    dlog,
    skip,
    bounds,
    xb,
    gb,
    sb,
    cx,
    cs,
    raw,
    gain,
    edge,
    from_left,
    from_right,
    xp,
    sp,
    xd,
    cv,
    bt,
    late,
    gm,
    mk,
    kp,
    st,
    yv,
    infl,
    sg,
    dsend,
    drecv,
    sbuf,
    rbuf,
    ebuf,
    fbuf,
    hbuf,
    ob,
    in_sem,
    out_sem,
    halo_send,
    halo_recv,
    fac_sem,
    tile_sem,
    back_sem,
    head_sem,
    line_sem,
    near_sem,
    mate_sem,
):
    seq = lax.axis_index("seq")
    head = lax.axis_index("head")
    tp = TILES // n
    fj = 1 if tp == 1 else PAIRS

    def load(i, src, dst):
        copy = pltpu.make_async_copy(src, dst, in_sem.at[i])
        copy.start()
        return copy

    load_bias = load(7, bias_hbm, bias)
    load_dlog = load(8, dlog_hbm, dlog)
    load_bounds = load(9, bounds_hbm, bounds)
    load_skip = load(10, skip_hbm, skip)
    load_raw = load(0, raw_hbm, raw)
    load_s = load(1, s_hbm, sb)
    load_cs = load(2, cs_hbm, cs)
    load_x = load(3, x_hbm, xb)
    load_cx = load(4, cx_hbm, cx)
    load_g = load(5, g_hbm, gb)
    load_gain = load(6, gain_hbm, gain)

    lines = n // 4
    line = seq // 4
    place = lax.rem(seq, 4)
    across = (
        3 - place,
        lax.rem(place + 2, 4),
        place + 1 - 2 * lax.rem(place, 2),
        place,
    )

    def apart(d):
        return -min(d // 4, 4 - d // 4) - min(d % 4, 4 - d % 4)

    far_first = sorted(range(lines), key=apart)

    def to_peers(act):
        for at in across:
            for d in far_first:
                if at is not place or d > 0:
                    act(lax.rem(line + d, lines) * 4 + at)

    core = lax.rem(head, 2)
    ring = nh // 2
    mate = head + 1 - 2 * core
    up = lax.rem(head + 2, nh)
    down = lax.rem(head + nh - 2, nh)
    beside = (up, down) if ring > 2 else ((up,) if ring == 2 else ())

    barrier = pltpu.get_barrier_semaphore()
    right_dev = (lax.rem(seq + 1, n), head)
    left_dev = (lax.rem(seq + n - 1, n), head)
    greeted = [right_dev, left_dev]
    greeted += [(lax.rem(line + d, lines) * 4 + place, head) for d in range(1, lines)]
    greeted += [(line * 4 + at, head) for at in across[:3]]
    greeted += [(seq, other) for other in (mate,) + beside]
    for device in greeted:
        pl.semaphore_signal(barrier, inc=1, device_id=device, device_id_type=MESH)

    load_raw.wait()
    load_bias.wait()
    load_dlog.wait()
    sub = lax.broadcasted_iota(jnp.int32, (8, 128), 0)
    lane = lax.broadcasted_iota(jnp.int32, (1, 128), 1)
    left = lane < 64
    bias_col = jnp.zeros((8, 128), F32)
    rate_col = jnp.zeros((8, 128), F32)
    for h in range(8):
        bias_col = jnp.where(sub == h, bias[h], bias_col)
        rate_col = jnp.where(sub == h, dlog[h], rate_col)
    rate_col = -LOG2E * jnp.exp(rate_col)
    steps = []
    for b in range(2):
        z = raw[:, b * 128 : (b + 1) * 128].astype(F32) + bias_col
        small = jnp.exp(-jnp.abs(z))
        one = 1.0 + small
        exact = jnp.where(one == 1.0, small, jnp.log(one) * (small / jnp.where(one == 1.0, 1.0, one - 1.0)))
        steps.append(jnp.maximum(z, 0.0) + exact)
    decay = jnp.concatenate([steps[0] * rate_col, steps[1] * rate_col], axis=0)
    log_step = jnp.log(jnp.concatenate(steps, axis=0)) * LOG2E
    row_i = lax.broadcasted_iota(jnp.int32, (128, 128), 0)
    col_i = lax.broadcasted_iota(jnp.int32, (128, 128), 1)
    cum_f = mm_exact(decay, (row_i <= col_i).astype(F32))
    cum_b = mm_exact(decay, (row_i >= col_i).astype(F32))
    cums = (cum_f, cum_b)
    cols = jnp.transpose(jnp.concatenate([cum_f, cum_b, jnp.zeros((96, 128), F32)], axis=0))
    minus = (cum_f - log_step, cum_b - log_step)

    load_bounds.wait()
    base = seq * TOK

    def label(position):
        count = jnp.zeros_like(position)
        for i in range(8):
            count = count + (bounds[i] <= position).astype(jnp.int32)
        return count

    first = (label(base), label(base + 128))
    last = (label(base + 127), label(base + 255))
    prev = (label(base - 1), last[0])
    after = (first[1], label(base + 256))
    rows_of = [None, None]
    ends = []
    passes = []
    tails = []
    for s in range(2):
        ends.append([])
        passes.append([])
        tails.append([])
        for b in range(2):
            block = cums[s][b * 8 : (b + 1) * 8]
            end = jnp.broadcast_to(block[:, 127:128] if s == 0 else block[:, 0:1], (8, 128))
            ends[s].append(end)
            end_label = last[b] if s == 0 else first[b]
            outside = prev[b] if s == 0 else after[b]
            passes[s].append(jnp.where(end_label == outside, jnp.exp2(end), 0.0))
            labels = label(base + b * 128 + lax.broadcasted_iota(jnp.int32, (8, 128), 1))
            tails[s].append(
                jnp.where(
                    labels == end_label, jnp.exp2(end - minus[s][b * 8 : (b + 1) * 8]), 0.0
                )
            )
            rows_of[b] = labels[0:1]

    def spread(column, j):
        return jnp.where(left, column[2 * j : 2 * j + 1], column[2 * j + 1 : 2 * j + 2])

    for s in range(2):
        factor = passes[s][0] * passes[s][1]
        for j in range(PAIRS):
            dsend[s * PAIRS + j] = spread(factor, j)

    load_s.wait()
    load_cs.wait()
    load_x.wait()
    load_cx.wait()

    xp[PAD : PAD + TOK] = xb[...].astype(F32)
    sp[PAD : PAD + TOK] = sb[...].astype(F32)

    def conv(padded, taps, c, r0, rows, s):
        lanes = slice(c * 128, (c + 1) * 128)
        total = None
        for k in range(4):
            shift = -k if s == 0 else k
            term = (0.5 * taps[k : k + 1, lanes]) * padded[
                PAD + r0 + shift : PAD + r0 + shift + rows, lanes
            ]
            total = term if total is None else total + term
        return gate(total)

    def conv_x(j, r0, rows, s):
        v = conv(xp, cx, j, r0, rows, s)
        b = r0 // 128
        r = r0 - b * 128
        xd[s * 2 + b, j, r : r + rows] = jnp.where(left, v, 0.0).astype(BF16)
        xd[s * 2 + b, j, 128 + r : 128 + r + rows] = jnp.where(left, 0.0, v).astype(BF16)

    def conv_s(c, r0, rows, s):
        v = conv(sp, cs, c, r0, rows, s)
        b = r0 // 128
        r = r0 - b * 128
        cv[s * 2 + b, c, r : r + rows] = v.astype(BF16)

    inner = (
        (0, ((16, 48), (64, 64), (128, 64), (192, 64))),
        (1, ((0, 64), (64, 64), (128, 64), (192, 48))),
    )
    edges = ((0, 0), (1, TOK - 16))
    for c in range(2):
        for s, chunks in inner:
            for r0, rows in chunks:
                conv_s(c, r0, rows, s)
    for j in range(PAIRS):
        for s, chunks in inner:
            for r0, rows in chunks:
                conv_x(j, r0, rows, s)

    def block_state(s, b, j):
        q = s * 2 + b
        scaled = jnp.concatenate(
            [bt[q] * tails[s][b][2 * j + k : 2 * j + k + 1] for k in range(2)], axis=1
        ).astype(BF16)
        return mm(scaled, xd[q, j])

    for s in range(2):
        bt[s * 2 + 1 - s] = jnp.transpose(cv[s * 2 + 1 - s, 0].astype(F32))
        for j in range(PAIRS):
            late[s, j] = block_state(s, 1 - s, j)

    packed = ((xp, 0), (xp, 1), (xp, 2), (xp, 3), (sp, 0), (sp, 1))
    pad_row = jnp.zeros((1, 128), F32)
    for side, row in ((0, PAD + TOK - 3), (1, PAD)):
        rows = []
        for source, c in packed:
            rows += [source[row : row + 3, c * 128 : (c + 1) * 128], pad_row]
        rows.append(jnp.zeros((8, 128), F32))
        edge[side] = jnp.concatenate(rows, axis=0).astype(BF16)

    pl.semaphore_wait(barrier, len(greeted))

    halos = []
    for i, (src, dst, dev) in enumerate(
        ((edge.at[0], from_left, right_dev), (edge.at[1], from_right, left_dev))
    ):
        copy = pltpu.make_async_remote_copy(
            src_ref=src,
            dst_ref=dst,
            send_sem=halo_send.at[i],
            recv_sem=halo_recv.at[i],
            device_id=dev,
            device_id_type=MESH,
        )
        copy.start()
        halos.append(copy)

    for at in across[:3]:
        pl.semaphore_signal(
            line_sem, inc=1, device_id=(line * 4 + at, head), device_id_type=MESH
        )
    for other in beside:
        pl.semaphore_signal(near_sem, inc=1, device_id=(seq, other), device_id_type=MESH)
    for s in range(2):
        for b in range(2):
            outside = prev[b] if s == 0 else after[b]
            tok = label(base + b * 128 + row_i)
            order = row_i >= col_i if s == 0 else row_i <= col_i
            mk[s * 2 + b] = jnp.where((tok == rows_of[b]) & order, 0.0, NEG)
            kp[s * 2 + b] = jnp.where(tok == outside, 0.0, NEG)
    load_g.wait()
    for j in range(PAIRS):
        sg[j] = gate(0.5 * gb[:, j * 128 : (j + 1) * 128].astype(F32))

    pl.semaphore_wait(line_sem, 3)

    def send_factor(p):
        tile = p * tp
        strand = tile // 32
        at = strand * PAIRS + (lax.rem(tile, PAIRS) if fj == 1 else 0)
        pltpu.make_async_remote_copy(
            src_ref=dsend.at[pl.ds(at, fj)],
            dst_ref=drecv.at[seq],
            send_sem=fac_sem.at[0],
            recv_sem=fac_sem.at[1],
            device_id=(p, head),
            device_id_type=MESH,
        ).start()

    to_peers(send_factor)
    tile0 = seq * tp
    at0 = (tile0 // 32) * PAIRS + (lax.rem(tile0, PAIRS) if fj == 1 else 0)
    drecv[seq] = dsend[pl.ds(at0, fj)]

    has_left = seq > 0
    has_right = seq < n - 1
    arrivals = ((from_left, PAD - 3, has_left), (from_right, PAD + TOK, has_right))

    def finish(s):
        halos[s].wait_recv()
        ref, row, inside = arrivals[s]
        values = jnp.where(inside, ref[...].astype(F32), 0.0)
        for at, (target, c) in enumerate(packed):
            target[row : row + 3, c * 128 : (c + 1) * 128] = values[4 * at : 4 * at + 3]
        r0 = edges[s][1]
        for c in range(2):
            conv_s(c, r0, 16, s)
        for j in range(PAIRS):
            conv_x(j, r0, 16, s)
        bt[s * 3] = jnp.transpose(cv[s * 3, 0].astype(F32))
        for j in range(PAIRS):
            early = block_state(s, s, j)
            st[s, j] = early.astype(BF16)
            total = (spread(passes[s][1 - s], j) * early + late[s, j]).astype(BF16)
            for i in range(8):
                t = s * 32 + i * PAIRS + j
                sbuf[t // tp, t % tp] = total[i * 16 : (i + 1) * 16]

    def send_tile(p):
        pltpu.make_async_remote_copy(
            src_ref=sbuf.at[p],
            dst_ref=rbuf.at[seq],
            send_sem=tile_sem.at[0],
            recv_sem=tile_sem.at[1],
            device_id=(p, head),
            device_id_type=MESH,
        ).start()

    def send_unless_own(p):
        @pl.when(p != seq)
        def _():
            send_tile(p)

    def send_strand(s):
        if lines == 1:
            for p in range(s * 2, s * 2 + 2):
                send_unless_own(p)
            return
        half = lines // 2
        for at in across:
            for d in range(half):
                p = (s * half + lax.rem(line + d, half)) * 4 + at
                if at is place:
                    send_unless_own(p)
                else:
                    send_tile(p)

    @pl.when((place == 1) | (place == 2))
    def _():
        finish(0)
        finish(1)
        to_peers(send_tile)

    for end, order in ((0, (1, 0)), (3, (0, 1))):

        @pl.when(place == end)
        def _():
            for s in order:
                finish(s)
                send_strand(s)

    rbuf[seq] = sbuf[seq]

    if beside:
        pl.semaphore_wait(near_sem, len(beside))
        pl.semaphore_signal(mate_sem, inc=1, device_id=(seq, mate), device_id_type=MESH)

    def within(b):
        if b == 0:
            for q in range(4):
                gm[q] = mm_nt(cv[q, 1], cv[q, 0])
        for j in range(PAIRS):
            total = None
            for s in range(2):
                q = s * 2 + b
                wide = []
                parts = []
                for k in range(2):
                    h = 2 * j + k
                    at = s * 16 + b * 8 + h
                    column = jnp.broadcast_to(cols[:, at : at + 1], (128, 128))
                    wide.append(column)
                    row = minus[s][b * 8 + h : b * 8 + h + 1]
                    parts.append((jnp.exp2(column - row + mk[q]) * gm[q]).astype(BF16))
                values = xd[q, j]
                term = mm(jnp.concatenate(parts, axis=1), values)
                sk = jnp.where(left, skip[2 * j], skip[2 * j + 1])
                term = term + sk * (values[:128].astype(F32) + values[128:].astype(F32))
                flow = jnp.exp2(jnp.where(left, wide[0], wide[1]) + kp[q])
                if b != s:
                    term = term + flow * mm(cv[q, 1], st[s, j])
                    flow = flow * spread(passes[s][s], j)
                infl[s, j, b * 128 : (b + 1) * 128] = flow
                total = term if total is None else total + term
            yv[j, b * 128 : (b + 1) * 128] = total

    load_skip.wait()
    within(0)
    within(1)

    def wait_all(sem, ref):
        pltpu.make_async_copy(ref, ref, sem).wait()

    wait_all(fac_sem.at[1], drecv.at[pl.ds(0, n - 1)])
    wait_all(tile_sem.at[1], rbuf.at[pl.ds(0, n - 1)])

    reverse = tile0 >= 32

    def scan(i, carry):
        k = jnp.where(reverse, n - 1 - i, i)
        new = []
        for t in range(tp):
            ebuf[k, t] = carry[t].astype(BF16)
            new.append(drecv[k, t % fj] * carry[t] + rbuf[k, t].astype(F32))
        return tuple(new)

    lax.fori_loop(
        0, n, scan, tuple(jnp.zeros((16, 128), F32) for _ in range(tp)), unroll=8
    )

    def send_back(p):
        pltpu.make_async_remote_copy(
            src_ref=ebuf.at[p],
            dst_ref=fbuf.at[seq],
            send_sem=back_sem.at[0],
            recv_sem=back_sem.at[1],
            device_id=(p, head),
            device_id_type=MESH,
        ).start()

    def toward(p):
        @pl.when(p != seq)
        def _():
            send_back(p)

    for d in reversed(far_first):
        toward(d * 4)
    for at in range(1, 4):
        for d in far_first:
            toward(lax.rem(line + d, lines) * 4 + at)

    fbuf[seq] = ebuf[seq]
    load_gain.wait()
    wait_all(back_sem.at[1], fbuf.at[pl.ds(0, n - 1)])

    squares = jnp.zeros((TOK, 128), F32)
    for j in range(PAIRS):
        y = yv[j]
        for s in range(2):
            pieces = []
            for i in range(8):
                t = s * 32 + i * PAIRS + j
                pieces.append(fbuf[t // tp, t % tp])
            entering = jnp.concatenate(pieces, axis=0)
            c_all = jnp.concatenate([cv[s * 2, 1], cv[s * 2 + 1, 1]], axis=0)
            y = y + infl[s, j] * mm(c_all, entering)
        mixed = y * sg[j]
        yv[j] = mixed * gain[:, j * 128 : (j + 1) * 128]
        squares = squares + mixed * mixed
    sums = jnp.concatenate(
        [
            jnp.sum(jnp.transpose(squares[b * 128 : (b + 1) * 128]), axis=0, keepdims=True)
            for b in range(2)
        ],
        axis=1,
    )
    hbuf[head] = sums

    def send_sums(d, carry):
        p = lax.rem(head + d, nh)
        pltpu.make_async_remote_copy(
            src_ref=hbuf.at[head],
            dst_ref=hbuf.at[head],
            send_sem=head_sem.at[0],
            recv_sem=head_sem.at[1],
            device_id=(seq, p),
            device_id_type=MESH,
        ).start()
        return carry

    if beside:
        pl.semaphore_wait(mate_sem, 1)
    lax.fori_loop(1, nh, send_sums, 0)
    wait_all(head_sem.at[1], hbuf.at[pl.ds(0, nh - 1)])
    total = hbuf[0]
    for p in range(1, nh):
        total = total + hbuf[p]
    scale = lax.rsqrt(total * (1.0 / channels) + 1e-5)
    for b in range(2):
        column = jnp.transpose(jnp.broadcast_to(scale[:, b * 128 : (b + 1) * 128], (128, 128)))
        for j in range(PAIRS):
            lanes = slice(j * 128, (j + 1) * 128)
            out_hbm[b * 128 : (b + 1) * 128, lanes] = (
                yv[j, b * 128 : (b + 1) * 128] * column
            ).astype(BF16)
    for copy in halos:
        copy.wait_send()
    wait_all(fac_sem.at[0], drecv.at[pl.ds(0, n - 1)])
    wait_all(tile_sem.at[0], rbuf.at[pl.ds(0, n - 1)])
    wait_all(back_sem.at[0], fbuf.at[pl.ds(0, n - 1)])
    wait_all(head_sem.at[0], hbuf.at[pl.ds(0, nh - 1)])


def body(
    inputs,
    gating,
    state_proj,
    conv_inputs,
    conv_state,
    step_raw,
    step_bias,
    decay_log,
    skip_gain,
    norm_gain,
    boundaries,
):
    n = lax.axis_size("seq")
    nh = lax.axis_size("head")
    tp = TILES // n
    fj = 1 if tp == 1 else PAIRS
    width = inputs.shape[1]
    hbm = pl.BlockSpec(memory_space=pltpu.HBM)
    smem = pltpu.SMEM
    vm = pltpu.VMEM
    dma = pltpu.SemaphoreType.DMA
    return pl.pallas_call(
        functools.partial(kernel, n, nh, width * nh),
        out_shape=pltpu.VMEM(inputs.shape, BF16),
        in_specs=[hbm] * 11,
        out_specs=pl.BlockSpec(memory_space=pltpu.VMEM),
        scratch_shapes=[
            smem((8,), F32),
            smem((8,), F32),
            smem((8,), F32),
            smem((8,), jnp.int32),
            vm((TOK, 512), BF16),
            vm((TOK, 512), BF16),
            vm((TOK, 256), BF16),
            vm((4, 512), F32),
            vm((4, 256), F32),
            vm((8, TOK), BF16),
            vm((1, 512), F32),
            vm((2, 32, 128), BF16),
            vm((32, 128), BF16),
            vm((32, 128), BF16),
            vm((TOK + 2 * PAD, 512), F32),
            vm((TOK + 2 * PAD, 256), F32),
            vm((4, PAIRS, 256, 128), BF16),
            vm((4, 2, 128, 128), BF16),
            vm((4, 128, 128), F32),
            vm((2, PAIRS, 128, 128), F32),
            vm((4, 128, 128), F32),
            vm((4, 128, 128), F32),
            vm((4, 128, 128), F32),
            vm((2, PAIRS, 128, 128), BF16),
            vm((PAIRS, TOK, 128), F32),
            vm((2, PAIRS, TOK, 128), F32),
            vm((PAIRS, TOK, 128), F32),
            vm((2 * PAIRS, 1, 128), F32),
            vm((n, fj, 1, 128), F32),
            vm((n, tp, 16, 128), BF16),
            vm((n, tp, 16, 128), BF16),
            vm((n, tp, 16, 128), BF16),
            vm((n, tp, 16, 128), BF16),
            vm((nh, 1, TOK), F32),
            vm((TOK, 512), BF16),
            dma((11,)),
            dma,
            dma((4,)),
            dma((4,)),
            dma((2,)),
            dma((2,)),
            dma((2,)),
            dma((2,)),
            pltpu.SemaphoreType.REGULAR,
            pltpu.SemaphoreType.REGULAR,
            pltpu.SemaphoreType.REGULAR,
        ],
        compiler_params=pltpu.CompilerParams(
            collective_id=0, has_side_effects=True, vmem_limit_bytes=56 * 1024 * 1024
        ),
        cost_estimate=pl.CostEstimate(
            flops=400_000_000, bytes_accessed=1_000_000, transcendentals=1_000_000
        ),
    )(
        inputs,
        gating,
        state_proj,
        conv_inputs,
        conv_state,
        step_raw,
        norm_gain.reshape(1, width),
        step_bias,
        decay_log,
        skip_gain,
        boundaries,
    )


def solution(mesh):
    placed = (
        P("seq", "head"),
        P("seq", "head"),
        P("seq", None),
        P(None, "head"),
        P(),
        P("head", "seq"),
        P("head"),
        P("head"),
        P("head"),
        P("head"),
        P(),
    )
    return jax.shard_map(
        body, mesh=mesh, in_specs=placed, out_specs=P("seq", "head"), check_vma=False
    )
```

```python
import functools

import jax
import jax.numpy as jnp
from jax import lax
from jax.experimental import pallas as pl
from jax.experimental.pallas import tpu as pltpu
from jax.sharding import PartitionSpec as P

MESH = pl.DeviceIdType.MESH
LOG2E = 1.4426950408889634
NEG = -1e30
F32 = jnp.float32
BF16 = jnp.bfloat16
TOK = 256
GROUP = 128
PAIRS = 4
TILES = 64
PAD = 8


def mm(a, b):
    return lax.dot_general(a, b, (((1,), (0,)), ((), ())), preferred_element_type=F32)


def mm_nt(a, b):
    return lax.dot_general(a, b, (((1,), (1,)), ((), ())), preferred_element_type=F32)


def mm_exact(a, b):
    return lax.dot_general(
        a, b, (((1,), (0,)), ((), ())), preferred_element_type=F32, precision=lax.Precision.HIGHEST
    )


def gate(half):
    return half + half * jnp.tanh(half)


def kernel(
    n,
    nh,
    channels,
    x_hbm,
    g_hbm,
    s_hbm,
    cx_hbm,
    cs_hbm,
    raw_hbm,
    gain_hbm,
    bias_hbm,
    dlog_hbm,
    skip_hbm,
    bounds_hbm,
    out_hbm,
    bias,
    dlog,
    skip,
    bounds,
    xb,
    gb,
    sb,
    cx,
    cs,
    raw,
    gain,
    edge,
    from_left,
    from_right,
    xp,
    sp,
    xd,
    cv,
    bt,
    late,
    gm,
    mk,
    kp,
    st,
    yv,
    infl,
    sg,
    dsend,
    drecv,
    sbuf,
    rbuf,
    ebuf,
    fbuf,
    hbuf,
    ob,
    in_sem,
    out_sem,
    halo_send,
    halo_recv,
    fac_sem,
    tile_sem,
    back_sem,
    head_sem,
    line_sem,
    near_sem,
    mate_sem,
):
    seq = lax.axis_index("seq")
    head = lax.axis_index("head")
    tp = TILES // n
    fj = 1 if tp == 1 else PAIRS

    lines = n // 4
    line = seq // 4
    place = lax.rem(seq, 4)
    across = (
        3 - place,
        lax.rem(place + 2, 4),
        place + 1 - 2 * lax.rem(place, 2),
        place,
    )

    def apart(d):
        return -min(d // 4, 4 - d // 4) - min(d % 4, 4 - d % 4)

    far_first = sorted(range(lines), key=apart)

    def to_peers(act):
        for at in across:
            for d in far_first:
                if at is not place or d > 0:
                    act(lax.rem(line + d, lines) * 4 + at)

    core = lax.rem(head, 2)
    ring = nh // 2
    mate = head + 1 - 2 * core
    up = lax.rem(head + 2, nh)
    down = lax.rem(head + nh - 2, nh)
    beside = (up, down) if ring > 2 else ((up,) if ring == 2 else ())

    barrier = pltpu.get_barrier_semaphore()
    right_dev = (lax.rem(seq + 1, n), head)
    left_dev = (lax.rem(seq + n - 1, n), head)
    greeted = [right_dev, left_dev]
    greeted += [(lax.rem(line + d, lines) * 4 + place, head) for d in range(1, lines)]
    greeted += [(line * 4 + at, head) for at in across[:3]]
    greeted += [(seq, other) for other in (mate,) + beside]
    for device in greeted:
        pl.semaphore_signal(barrier, inc=1, device_id=device, device_id_type=MESH)

    def load(i, src, dst):
        copy = pltpu.make_async_copy(src, dst, in_sem.at[i])
        copy.start()
        return copy

    load_bias = load(7, bias_hbm, bias)
    load_dlog = load(8, dlog_hbm, dlog)
    load_bounds = load(9, bounds_hbm, bounds)
    load_skip = load(10, skip_hbm, skip)
    load_raw = load(0, raw_hbm, raw)
    load_s = load(1, s_hbm, sb)
    load_cs = load(2, cs_hbm, cs)
    load_x = load(3, x_hbm, xb)
    load_cx = load(4, cx_hbm, cx)
    load_g = load(5, g_hbm, gb)
    load_gain = load(6, gain_hbm, gain)

    load_raw.wait()
    load_bias.wait()
    load_dlog.wait()
    sub = lax.broadcasted_iota(jnp.int32, (8, 128), 0)
    lane = lax.broadcasted_iota(jnp.int32, (1, 128), 1)
    left = lane < 64
    bias_col = jnp.zeros((8, 128), F32)
    rate_col = jnp.zeros((8, 128), F32)
    for h in range(8):
        bias_col = jnp.where(sub == h, bias[h], bias_col)
        rate_col = jnp.where(sub == h, dlog[h], rate_col)
    rate_col = -LOG2E * jnp.exp(rate_col)
    steps = []
    for b in range(2):
        z = raw[:, b * 128 : (b + 1) * 128].astype(F32) + bias_col
        small = jnp.exp(-jnp.abs(z))
        one = 1.0 + small
        exact = jnp.where(one == 1.0, small, jnp.log(one) * (small / jnp.where(one == 1.0, 1.0, one - 1.0)))
        steps.append(jnp.maximum(z, 0.0) + exact)
    decay = jnp.concatenate([steps[0] * rate_col, steps[1] * rate_col], axis=0)
    log_step = jnp.log(jnp.concatenate(steps, axis=0)) * LOG2E
    row_i = lax.broadcasted_iota(jnp.int32, (128, 128), 0)
    col_i = lax.broadcasted_iota(jnp.int32, (128, 128), 1)
    cum_f = mm_exact(decay, (row_i <= col_i).astype(F32))
    cum_b = mm_exact(decay, (row_i >= col_i).astype(F32))
    cums = (cum_f, cum_b)
    cols = jnp.transpose(jnp.concatenate([cum_f, cum_b, jnp.zeros((96, 128), F32)], axis=0))
    minus = (cum_f - log_step, cum_b - log_step)

    load_bounds.wait()
    base = seq * TOK

    def label(position):
        count = jnp.zeros_like(position)
        for i in range(8):
            count = count + (bounds[i] <= position).astype(jnp.int32)
        return count

    first = (label(base), label(base + 128))
    last = (label(base + 127), label(base + 255))
    prev = (label(base - 1), last[0])
    after = (first[1], label(base + 256))
    rows_of = [None, None]
    ends = []
    passes = []
    tails = []
    for s in range(2):
        ends.append([])
        passes.append([])
        tails.append([])
        for b in range(2):
            block = cums[s][b * 8 : (b + 1) * 8]
            end = jnp.broadcast_to(block[:, 127:128] if s == 0 else block[:, 0:1], (8, 128))
            ends[s].append(end)
            end_label = last[b] if s == 0 else first[b]
            outside = prev[b] if s == 0 else after[b]
            passes[s].append(jnp.where(end_label == outside, jnp.exp2(end), 0.0))
            labels = label(base + b * 128 + lax.broadcasted_iota(jnp.int32, (8, 128), 1))
            tails[s].append(
                jnp.where(
                    labels == end_label, jnp.exp2(end - minus[s][b * 8 : (b + 1) * 8]), 0.0
                )
            )
            rows_of[b] = labels[0:1]

    def spread(column, j):
        return jnp.where(left, column[2 * j : 2 * j + 1], column[2 * j + 1 : 2 * j + 2])

    for s in range(2):
        factor = passes[s][0] * passes[s][1]
        for j in range(PAIRS):
            dsend[s * PAIRS + j] = spread(factor, j)

    load_s.wait()
    load_cs.wait()
    load_x.wait()
    load_cx.wait()

    xp[PAD : PAD + TOK] = xb[...].astype(F32)
    sp[PAD : PAD + TOK] = sb[...].astype(F32)

    def conv(padded, taps, c, r0, rows, s):
        lanes = slice(c * 128, (c + 1) * 128)
        total = None
        for k in range(4):
            shift = -k if s == 0 else k
            term = (0.5 * taps[k : k + 1, lanes]) * padded[
                PAD + r0 + shift : PAD + r0 + shift + rows, lanes
            ]
            total = term if total is None else total + term
        return gate(total)

    def conv_x(j, r0, rows, s):
        v = conv(xp, cx, j, r0, rows, s)
        b = r0 // 128
        r = r0 - b * 128
        xd[s * 2 + b, j, r : r + rows] = jnp.where(left, v, 0.0).astype(BF16)
        xd[s * 2 + b, j, 128 + r : 128 + r + rows] = jnp.where(left, 0.0, v).astype(BF16)

    def conv_s(c, r0, rows, s):
        v = conv(sp, cs, c, r0, rows, s)
        b = r0 // 128
        r = r0 - b * 128
        cv[s * 2 + b, c, r : r + rows] = v.astype(BF16)

    inner = (
        (0, ((16, 48), (64, 64), (128, 64), (192, 64))),
        (1, ((0, 64), (64, 64), (128, 64), (192, 48))),
    )
    edges = ((0, 0), (1, TOK - 16))
    for c in range(2):
        for s, chunks in inner:
            for r0, rows in chunks:
                conv_s(c, r0, rows, s)
    for j in range(PAIRS):
        for s, chunks in inner:
            for r0, rows in chunks:
                conv_x(j, r0, rows, s)

    def block_state(s, b, j):
        q = s * 2 + b
        scaled = jnp.concatenate(
            [bt[q] * tails[s][b][2 * j + k : 2 * j + k + 1] for k in range(2)], axis=1
        ).astype(BF16)
        return mm(scaled, xd[q, j])

    for s in range(2):
        bt[s * 2 + 1 - s] = jnp.transpose(cv[s * 2 + 1 - s, 0].astype(F32))
        for j in range(PAIRS):
            late[s, j] = block_state(s, 1 - s, j)

    packed = ((xp, 0), (xp, 1), (xp, 2), (xp, 3), (sp, 0), (sp, 1))
    pad_row = jnp.zeros((1, 128), F32)
    for side, row in ((0, PAD + TOK - 3), (1, PAD)):
        rows = []
        for source, c in packed:
            rows += [source[row : row + 3, c * 128 : (c + 1) * 128], pad_row]
        rows.append(jnp.zeros((8, 128), F32))
        edge[side] = jnp.concatenate(rows, axis=0).astype(BF16)

    pl.semaphore_wait(barrier, len(greeted))

    halos = []
    for i, (src, dst, dev) in enumerate(
        ((edge.at[0], from_left, right_dev), (edge.at[1], from_right, left_dev))
    ):
        copy = pltpu.make_async_remote_copy(
            src_ref=src,
            dst_ref=dst,
            send_sem=halo_send.at[i],
            recv_sem=halo_recv.at[i],
            device_id=dev,
            device_id_type=MESH,
        )
        copy.start()
        halos.append(copy)

    for at in across[:3]:
        pl.semaphore_signal(
            line_sem, inc=1, device_id=(line * 4 + at, head), device_id_type=MESH
        )
    for other in beside:
        pl.semaphore_signal(near_sem, inc=1, device_id=(seq, other), device_id_type=MESH)
    for s in range(2):
        for b in range(2):
            outside = prev[b] if s == 0 else after[b]
            tok = label(base + b * 128 + row_i)
            order = row_i >= col_i if s == 0 else row_i <= col_i
            mk[s * 2 + b] = jnp.where((tok == rows_of[b]) & order, 0.0, NEG)
            kp[s * 2 + b] = jnp.where(tok == outside, 0.0, NEG)
    load_g.wait()
    for j in range(PAIRS):
        sg[j] = gate(0.5 * gb[:, j * 128 : (j + 1) * 128].astype(F32))

    pl.semaphore_wait(line_sem, 3)

    def send_factor(p):
        tile = p * tp
        strand = tile // 32
        at = strand * PAIRS + (lax.rem(tile, PAIRS) if fj == 1 else 0)
        pltpu.make_async_remote_copy(
            src_ref=dsend.at[pl.ds(at, fj)],
            dst_ref=drecv.at[seq],
            send_sem=fac_sem.at[0],
            recv_sem=fac_sem.at[1],
            device_id=(p, head),
            device_id_type=MESH,
        ).start()

    to_peers(send_factor)
    tile0 = seq * tp
    at0 = (tile0 // 32) * PAIRS + (lax.rem(tile0, PAIRS) if fj == 1 else 0)
    drecv[seq] = dsend[pl.ds(at0, fj)]

    has_left = seq > 0
    has_right = seq < n - 1
    arrivals = ((from_left, PAD - 3, has_left), (from_right, PAD + TOK, has_right))

    def finish(s):
        halos[s].wait_recv()
        ref, row, inside = arrivals[s]
        values = jnp.where(inside, ref[...].astype(F32), 0.0)
        for at, (target, c) in enumerate(packed):
            target[row : row + 3, c * 128 : (c + 1) * 128] = values[4 * at : 4 * at + 3]
        r0 = edges[s][1]
        for c in range(2):
            conv_s(c, r0, 16, s)
        for j in range(PAIRS):
            conv_x(j, r0, 16, s)
        bt[s * 3] = jnp.transpose(cv[s * 3, 0].astype(F32))
        for j in range(PAIRS):
            early = block_state(s, s, j)
            st[s, j] = early.astype(BF16)
            total = (spread(passes[s][1 - s], j) * early + late[s, j]).astype(BF16)
            for i in range(8):
                t = s * 32 + i * PAIRS + j
                sbuf[t // tp, t % tp] = total[i * 16 : (i + 1) * 16]

    def send_tile(p):
        pltpu.make_async_remote_copy(
            src_ref=sbuf.at[p],
            dst_ref=rbuf.at[seq],
            send_sem=tile_sem.at[0],
            recv_sem=tile_sem.at[1],
            device_id=(p, head),
            device_id_type=MESH,
        ).start()

    def send_unless_own(p):
        @pl.when(p != seq)
        def _():
            send_tile(p)

    def send_strand(s):
        if lines == 1:
            for p in range(s * 2, s * 2 + 2):
                send_unless_own(p)
            return
        half = lines // 2
        for at in across:
            for d in range(half):
                p = (s * half + lax.rem(line + d, half)) * 4 + at
                if at is place:
                    send_unless_own(p)
                else:
                    send_tile(p)

    @pl.when((place == 1) | (place == 2))
    def _():
        finish(0)
        finish(1)
        to_peers(send_tile)

    for end, order in ((0, (1, 0)), (3, (0, 1))):

        @pl.when(place == end)
        def _():
            for s in order:
                finish(s)
                send_strand(s)

    rbuf[seq] = sbuf[seq]

    if beside:
        pl.semaphore_wait(near_sem, len(beside))
        pl.semaphore_signal(mate_sem, inc=1, device_id=(seq, mate), device_id_type=MESH)

    def within(b):
        if b == 0:
            for q in range(4):
                gm[q] = mm_nt(cv[q, 1], cv[q, 0])
        for j in range(PAIRS):
            total = None
            for s in range(2):
                q = s * 2 + b
                wide = []
                parts = []
                for k in range(2):
                    h = 2 * j + k
                    at = s * 16 + b * 8 + h
                    column = jnp.broadcast_to(cols[:, at : at + 1], (128, 128))
                    wide.append(column)
                    row = minus[s][b * 8 + h : b * 8 + h + 1]
                    parts.append((jnp.exp2(column - row + mk[q]) * gm[q]).astype(BF16))
                values = xd[q, j]
                term = mm(jnp.concatenate(parts, axis=1), values)
                sk = jnp.where(left, skip[2 * j], skip[2 * j + 1])
                term = term + sk * (values[:128].astype(F32) + values[128:].astype(F32))
                flow = jnp.exp2(jnp.where(left, wide[0], wide[1]) + kp[q])
                if b != s:
                    term = term + flow * mm(cv[q, 1], st[s, j])
                    flow = flow * spread(passes[s][s], j)
                infl[s, j, b * 128 : (b + 1) * 128] = flow
                total = term if total is None else total + term
            yv[j, b * 128 : (b + 1) * 128] = total

    load_skip.wait()
    within(0)
    within(1)

    def wait_all(sem, ref):
        pltpu.make_async_copy(ref, ref, sem).wait()

    wait_all(fac_sem.at[1], drecv.at[pl.ds(0, n - 1)])
    wait_all(tile_sem.at[1], rbuf.at[pl.ds(0, n - 1)])

    reverse = tile0 >= 32

    def scan(i, carry):
        k = jnp.where(reverse, n - 1 - i, i)
        new = []
        for t in range(tp):
            ebuf[k, t] = carry[t].astype(BF16)
            new.append(drecv[k, t % fj] * carry[t] + rbuf[k, t].astype(F32))
        return tuple(new)

    lax.fori_loop(
        0, n, scan, tuple(jnp.zeros((16, 128), F32) for _ in range(tp)), unroll=8
    )

    def send_back(p):
        pltpu.make_async_remote_copy(
            src_ref=ebuf.at[p],
            dst_ref=fbuf.at[seq],
            send_sem=back_sem.at[0],
            recv_sem=back_sem.at[1],
            device_id=(p, head),
            device_id_type=MESH,
        ).start()

    def toward(p):
        @pl.when(p != seq)
        def _():
            send_back(p)

    for d in reversed(far_first):
        toward(d * 4)
    for at in range(1, 4):
        for d in far_first:
            toward(lax.rem(line + d, lines) * 4 + at)

    fbuf[seq] = ebuf[seq]
    load_gain.wait()
    wait_all(back_sem.at[1], fbuf.at[pl.ds(0, n - 1)])

    squares = jnp.zeros((TOK, 128), F32)
    for j in range(PAIRS):
        y = yv[j]
        for s in range(2):
            pieces = []
            for i in range(8):
                t = s * 32 + i * PAIRS + j
                pieces.append(fbuf[t // tp, t % tp])
            entering = jnp.concatenate(pieces, axis=0)
            c_all = jnp.concatenate([cv[s * 2, 1], cv[s * 2 + 1, 1]], axis=0)
            y = y + infl[s, j] * mm(c_all, entering)
        mixed = y * sg[j]
        yv[j] = mixed * gain[:, j * 128 : (j + 1) * 128]
        squares = squares + mixed * mixed
    sums = jnp.concatenate(
        [
            jnp.sum(jnp.transpose(squares[b * 128 : (b + 1) * 128]), axis=0, keepdims=True)
            for b in range(2)
        ],
        axis=1,
    )
    hbuf[head] = sums

    def send_sums(d, carry):
        p = lax.rem(head + d, nh)
        pltpu.make_async_remote_copy(
            src_ref=hbuf.at[head],
            dst_ref=hbuf.at[head],
            send_sem=head_sem.at[0],
            recv_sem=head_sem.at[1],
            device_id=(seq, p),
            device_id_type=MESH,
        ).start()
        return carry

    if beside:
        pl.semaphore_wait(mate_sem, 1)
    lax.fori_loop(1, nh, send_sums, 0)
    wait_all(head_sem.at[1], hbuf.at[pl.ds(0, nh - 1)])
    total = hbuf[0]
    for p in range(1, nh):
        total = total + hbuf[p]
    scale = lax.rsqrt(total * (1.0 / channels) + 1e-5)
    for b in range(2):
        column = jnp.transpose(jnp.broadcast_to(scale[:, b * 128 : (b + 1) * 128], (128, 128)))
        for j in range(PAIRS):
            lanes = slice(j * 128, (j + 1) * 128)
            out_hbm[b * 128 : (b + 1) * 128, lanes] = (
                yv[j, b * 128 : (b + 1) * 128] * column
            ).astype(BF16)
    for copy in halos:
        copy.wait_send()
    wait_all(fac_sem.at[0], drecv.at[pl.ds(0, n - 1)])
    wait_all(tile_sem.at[0], rbuf.at[pl.ds(0, n - 1)])
    wait_all(back_sem.at[0], fbuf.at[pl.ds(0, n - 1)])
    wait_all(head_sem.at[0], hbuf.at[pl.ds(0, nh - 1)])


def body(
    inputs,
    gating,
    state_proj,
    conv_inputs,
    conv_state,
    step_raw,
    step_bias,
    decay_log,
    skip_gain,
    norm_gain,
    boundaries,
):
    n = lax.axis_size("seq")
    nh = lax.axis_size("head")
    tp = TILES // n
    fj = 1 if tp == 1 else PAIRS
    width = inputs.shape[1]
    hbm = pl.BlockSpec(memory_space=pltpu.HBM)
    smem = pltpu.SMEM
    vm = pltpu.VMEM
    dma = pltpu.SemaphoreType.DMA
    return pl.pallas_call(
        functools.partial(kernel, n, nh, width * nh),
        out_shape=pltpu.VMEM(inputs.shape, BF16),
        in_specs=[hbm] * 11,
        out_specs=pl.BlockSpec(memory_space=pltpu.VMEM),
        scratch_shapes=[
            smem((8,), F32),
            smem((8,), F32),
            smem((8,), F32),
            smem((8,), jnp.int32),
            vm((TOK, 512), BF16),
            vm((TOK, 512), BF16),
            vm((TOK, 256), BF16),
            vm((4, 512), F32),
            vm((4, 256), F32),
            vm((8, TOK), BF16),
            vm((1, 512), F32),
            vm((2, 32, 128), BF16),
            vm((32, 128), BF16),
            vm((32, 128), BF16),
            vm((TOK + 2 * PAD, 512), F32),
            vm((TOK + 2 * PAD, 256), F32),
            vm((4, PAIRS, 256, 128), BF16),
            vm((4, 2, 128, 128), BF16),
            vm((4, 128, 128), F32),
            vm((2, PAIRS, 128, 128), F32),
            vm((4, 128, 128), F32),
            vm((4, 128, 128), F32),
            vm((4, 128, 128), F32),
            vm((2, PAIRS, 128, 128), BF16),
            vm((PAIRS, TOK, 128), F32),
            vm((2, PAIRS, TOK, 128), F32),
            vm((PAIRS, TOK, 128), F32),
            vm((2 * PAIRS, 1, 128), F32),
            vm((n, fj, 1, 128), F32),
            vm((n, tp, 16, 128), BF16),
            vm((n, tp, 16, 128), BF16),
            vm((n, tp, 16, 128), BF16),
            vm((n, tp, 16, 128), BF16),
            vm((nh, 1, TOK), F32),
            vm((TOK, 512), BF16),
            dma((11,)),
            dma,
            dma((4,)),
            dma((4,)),
            dma((2,)),
            dma((2,)),
            dma((2,)),
            dma((2,)),
            pltpu.SemaphoreType.REGULAR,
            pltpu.SemaphoreType.REGULAR,
            pltpu.SemaphoreType.REGULAR,
        ],
        compiler_params=pltpu.CompilerParams(
            collective_id=0, has_side_effects=True, vmem_limit_bytes=56 * 1024 * 1024
        ),
        cost_estimate=pl.CostEstimate(
            flops=400_000_000, bytes_accessed=1_000_000, transcendentals=1_000_000
        ),
    )(
        inputs,
        gating,
        state_proj,
        conv_inputs,
        conv_state,
        step_raw,
        norm_gain.reshape(1, width),
        step_bias,
        decay_log,
        skip_gain,
        boundaries,
    )


def solution(mesh):
    placed = (
        P("seq", "head"),
        P("seq", "head"),
        P("seq", None),
        P(None, "head"),
        P(),
        P("head", "seq"),
        P("head"),
        P("head"),
        P("head"),
        P("head"),
        P(),
    )
    return jax.shard_map(
        body, mesh=mesh, in_specs=placed, out_specs=P("seq", "head"), check_vma=False
    )
```
